512 devices in a mesh: slab: 32 (over y, x), band: 16 (over z, core).
Axes of the slice: x: 4, y: 8, z: 8, core: 2. Of those that a mesh axis runs over, the one named last changes fastest.
Arguments:
- projections: bfloat16 [4096, 18, 512], P('band', None, 'slab'), may hold values from -0.09375 to 0.09375
- occupation: float32 [4096], P('band'), may hold values from 0.5 to 2
- augment_tables: bfloat16 [2, 171, 48, 2304], P(None, None, 'band'), may hold values from -0.01953125 to 0.01953125
- box_root: int32 [512], P('slab'), may hold values from 0 to 575, as said below
- box_xy: int32 [512], P('slab'), may hold values from 0 to 2303
- species: int32 [512], P('slab'), may hold values from 0 to 1
- potential: float32 [576, 2304], P('slab'), may hold values from -6 to 6
Outputs:
- aug_density: float32 [576, 2304], P('slab')
- integrals: float32 [171, 512], P(None, ('slab', 'band'))
The draws below stay inside these ranges and needn't reach their ends.
Inputs may be any that keep to these rules, and one draw needn't show every extreme that they name: `box_root`: atom a's root lies in the planes of the slab that stores it, from (a // 16) * 18 to (a // 16) * 18 + 17; in every slab some atom starts at the slab's first plane and some at its last.
All inputs are finite; a program needn't handle non-finite values.
Results may differ from the reference program's by a relative error of at most 0.0031.
Values may be sent and summed in bfloat16 or wider, within the bound.
A program may use at most 64 MiB of HBM per device.

```python
import math
import jax
import jax.numpy as jnp
import numpy as np
from jax import lax

NH = 18
NSP = 2
BOX = 48
GX = 48
CZ = 18
ATOM_DEV = 16
GXY = 2304
NPAIR = 171
NB = 4096
NAT = 512
NZ = 576
N_SLAB = 32


def draw_box_root(key, part):
    key = jax.random.fold_in(key, 7)
    offsets = jax.random.randint(key, (N_SLAB, ATOM_DEV), 0, CZ)
    column = lax.broadcasted_iota(jnp.int32, (N_SLAB, ATOM_DEV), 1)
    offsets = jnp.where(column == 0, 0, jnp.where(column == ATOM_DEV - 1, CZ - 1, offsets))
    base = lax.broadcasted_iota(jnp.int32, (N_SLAB, ATOM_DEV), 0) * CZ
    return (base + offsets).reshape(N_SLAB * ATOM_DEV).astype(jnp.int32)


def plant(result, key, smallest, high):
    extent = result.shape
    place = [jax.random.randint(jax.random.fold_in(key, axis), (), 0, extent[axis]) for axis in range(len(extent))]
    result = result.at[tuple(place)].set(smallest)
    longest = extent.index(max(extent))
    place[longest] = (place[longest] + 1) % extent[longest]
    return result.at[tuple(place)].set(high)


def shard_levels(key, shape, pieces, smallest, largest):
    gain = 1.0
    for axis_at, shards_of in pieces:
        draws = jax.random.uniform(jax.random.fold_in(jax.random.fold_in(key, 6), axis_at), (shards_of,), jnp.float32, smallest / len(pieces), largest / len(pieces))
        gain = gain * jnp.repeat(jnp.exp(draws), shape[axis_at] // shards_of).reshape((-1,) + (1,) * (len(shape) - 1 - axis_at))
    return gain


def gaussian(key, extent, spread, bound, shards=(), dtype=jnp.bfloat16):
    array = spread * jax.random.normal(key, extent, jnp.float32)
    if shards:
        array = array * shard_levels(key, extent, shards, -0.22, 0.18)
    return jnp.clip(array, -bound, bound).astype(dtype)


def setup_inputs(seed: int = 0) -> dict:
    key_list = jax.random.split(jax.random.key(seed), 8)
    return {
        "projections": gaussian(key_list[0], (NB, NH, NAT), NB ** -0.5, 0.09375, ((0, 16), (2, 32))),
        "occupation": jnp.clip(jnp.exp(math.log(2.0) - 1.3862944 * jax.random.uniform(key_list[1], (NB,), jnp.float32) ** shard_levels(key_list[1], (NB,), ((0, 16),), -0.2, 0.2)), 0.5, 2.0),
        "augment_tables": gaussian(key_list[2], (NSP, NPAIR, BOX, GXY), (BOX * GXY) ** -0.5, 0.01953125, ((2, 16),)),
        "box_root": draw_box_root(jax.random.fold_in(key_list[7], 71), 0),
        "box_xy": plant(jax.random.randint(key_list[4], (NAT,), 0, GXY), jax.random.fold_in(key_list[4], 1), 0, GXY - 1).astype(jnp.int32),
        "species": plant(jax.random.randint(key_list[5], (NAT,), 0, NSP), jax.random.fold_in(key_list[5], 1), 0, NSP - 1).astype(jnp.int32),
        "potential": gaussian(key_list[6], (NZ, GXY), 1.0, 6.0, ((0, 32),), jnp.float32),
    }


def grid_columns(anchor, side):
    box_col = jnp.arange(side * side).astype(jnp.int32)
    return ((anchor[:, None] // side + box_col[None, :] // side) % side) * side + (anchor[:, None] + box_col[None, :]) % side


def box_columns(anchor, side):
    grid_col = jnp.arange(side * side).astype(jnp.int32)
    return ((grid_col[None, :] // side - anchor[:, None] // side) % side) * side + (grid_col[None, :] - anchor[:, None]) % side


def reference(projections, occupation, augment_tables, box_root, box_xy, species, potential):
    row_index, col_index = np.triu_indices(NH)
    factor = np.where(row_index == col_index, 1.0, 2.0)
    weighted = projections.astype(jnp.float32) * occupation[:, None, None]
    outer_sums = jnp.einsum("nia,nja->ija", weighted, projections.astype(jnp.float32), precision=lax.Precision.HIGHEST)
    becsum = outer_sums[row_index, col_index] * jnp.asarray(factor, jnp.float32)[:, None]
    packed = becsum.astype(jnp.bfloat16)
    flat_tables = augment_tables.reshape(NSP * NPAIR, BOX * GXY)
    rounded = potential.astype(jnp.bfloat16)
    depth = jnp.arange(BOX).astype(jnp.int32)
    block_sums = packed.reshape(NPAIR, N_SLAB, ATOM_DEV).transpose(1, 0, 2)
    block_root = box_root.reshape(N_SLAB, ATOM_DEV)
    block_xy = box_xy.reshape(N_SLAB, ATOM_DEV)
    block_species = species.reshape(N_SLAB, ATOM_DEV)

    def one_block(density, inputs):
        sums, roots, anchors, kinds = inputs
        masked = [jnp.where(kinds[None, :] == species_id, sums, jnp.zeros_like(sums)) for species_id in range(NSP)]
        stacked = jnp.concatenate(masked, axis=0)
        box_terms = jnp.dot(stacked.T, flat_tables, preferred_element_type=jnp.float32).reshape(ATOM_DEV, BOX, GXY)
        source = jnp.broadcast_to(box_columns(anchors, GX)[:, None, :], (ATOM_DEV, BOX, GXY))
        placed = jnp.take_along_axis(box_terms, source, axis=2)
        plane_ids = ((roots[:, None] + depth[None, :]) % NZ).reshape(-1).astype(jnp.int32)
        density = density + jax.ops.segment_sum(placed.reshape(ATOM_DEV * BOX, GXY), plane_ids, num_segments=NZ)
        rows = jnp.take(rounded, plane_ids, axis=0).reshape(ATOM_DEV, BOX, GXY)
        target = jnp.broadcast_to(grid_columns(anchors, GX)[:, None, :], (ATOM_DEV, BOX, GXY))
        box_values = jnp.take_along_axis(rows, target, axis=2).reshape(ATOM_DEV, BOX * GXY)
        projected = jnp.dot(box_values, flat_tables.T, preferred_element_type=jnp.float32).T
        integrals = jnp.zeros((NPAIR, ATOM_DEV), jnp.float32)
        for species_id in range(NSP):
            piece = projected[species_id * NPAIR:(species_id + 1) * NPAIR]
            integrals = integrals + jnp.where(kinds[None, :] == species_id, piece, jnp.zeros_like(piece))
        return density, integrals

    density, integrals = lax.scan(one_block, jnp.zeros((NZ, GXY), jnp.float32), (block_sums, block_root, block_xy, block_species))
    return density, integrals.transpose(1, 0, 2).reshape(NPAIR, NAT)
```

```python
import jax
import jax.numpy as jnp
from jax import lax
from jax.experimental import pallas as pl
from jax.experimental.pallas import tpu as pltpu
from jax.sharding import PartitionSpec as P

GX = 48
GXY = 2304
NH = 18
NPAIR = 171
DEPTH = 3
CZ = 18
ATOMS = 16
BAND = 16
SLAB = 32
PAD_P = 176
ROWS = 2 * PAD_P
OWNERS = 6
WIDE = GXY // OWNERS
WINDOW = 24
F32 = jnp.float32
BF16 = jnp.bfloat16
NT = (((1,), (1,)), ((), ()))


def iota(shape, axis):
    return lax.broadcasted_iota(jnp.int32, shape, axis)


def dot(a, b):
    return jnp.dot(a, b, preferred_element_type=F32)


def dot_nt(a, b):
    return lax.dot_general(a, b, NT, preferred_element_type=F32)


def split(x, terms):
    parts = []
    for _ in range(terms):
        part = x.astype(BF16)
        parts.append(part)
        x = x - part.astype(F32)
    return parts


def column(row):
    picked = jnp.where(iota((ATOMS, ATOMS), 0) == iota((ATOMS, ATOMS), 1), row.astype(F32), 0.0)
    return jnp.sum(picked, axis=1, keepdims=True).astype(jnp.int32)


def rotate(values, amount, left):
    amount = jnp.broadcast_to(amount, values.shape)
    for bit in range(12):
        step = 1 << bit
        turned = pltpu.roll(values, GXY - step if left else step, 1)
        values = jnp.where((amount & step) != 0, turned, values)
    return values


def remote(src, dst, send, recv, **where):
    return pltpu.make_async_remote_copy(
        src_ref=src,
        dst_ref=dst,
        send_sem=send,
        recv_sem=recv,
        device_id=where,
        device_id_type=pl.DeviceIdType.MESH,
    )


def kernel(
    pt, occ, root, xy, kind, pot, tab, dens, ints,
    raw, tables, bt, rs1, tt, pex, pout, pin, boxes, ext, rs3, st, p4, exq, ag, isnd, ircv,
    tab_sem, s1, r1, s2, r2, sp, rp, s3, r3, s4, r4, s5, r5, s6, r6,
):
    me = lax.axis_index("band")
    slab = lax.axis_index("slab")

    def peer(rel):
        return lax.rem(me + rel, BAND)

    barrier = pltpu.get_barrier_semaphore()

    def greet(rel, carry):
        pl.semaphore_signal(
            barrier, inc=1, device_id={"band": peer(rel)}, device_id_type=pl.DeviceIdType.MESH
        )
        return carry

    lax.fori_loop(1, BAND, greet, 0)
    for k in (1, 2, 3, SLAB - 3, SLAB - 2, SLAB - 1):
        pl.semaphore_signal(
            barrier, inc=1, device_id={"slab": lax.rem(slab + k, SLAB)},
            device_id_type=pl.DeviceIdType.MESH,
        )
    fetch = pltpu.make_async_copy(tab, raw.at[pl.ds(0, NPAIR)], tab_sem)
    fetch.start()

    p = pt[...]
    weighted = split(p.astype(F32) * occ[...], 2)
    gram = dot_nt(weighted[0], p) + dot_nt(weighted[1], p)
    size = NH * ATOMS
    same = (iota((size, size), 0) & 15) == (iota((size, size), 1) & 15)
    pair = iota((1, 256), 1)
    i_of = jnp.zeros((1, 256), jnp.int32)
    start = jnp.zeros((1, 256), jnp.int32)
    for i in range(1, NH):
        past = pair >= i * NH - i * (i - 1) // 2
        i_of = i_of + jnp.where(past, 1, 0)
        start = start + jnp.where(past, NH - i + 1, 0)
    j_of = pair - start + i_of
    pick_j = jnp.where((iota((size, 256), 0) >> 4) == j_of, 1.0, 0.0).astype(BF16)
    spread = jnp.zeros((size, 256), F32)
    for part in split(jnp.where(same, gram, 0.0), 3):
        spread = spread + dot(part, pick_j)
    partial = jnp.zeros((ATOMS, 256), F32)
    for i in range(NH):
        partial = partial + jnp.where(i_of == i, spread[i * ATOMS : (i + 1) * ATOMS], 0.0)
    partial = partial * jnp.where(i_of == j_of, 1.0, 2.0)
    for t in range(4):
        bt[t] = partial[t // 2 * 8 : t // 2 * 8 + 8, t % 2 * 128 : t % 2 * 128 + 128]

    pl.semaphore_wait(barrier, BAND - 1 + 6)

    def send1(t):
        return remote(bt.at[t], rs1.at[me], s1.at[t], r1.at[me], band=4 * t)

    for t in range(4):
        @pl.when(me != 4 * t)
        def _(t=t):
            send1(t).start()

        @pl.when(me == 4 * t)
        def _(t=t):
            rs1[me] = bt[t]

    pout[:, 0:GXY] = pot[0:16, :].astype(BF16)
    pex[...] = jnp.zeros(pex.shape, F32)
    for r in range(2):
        for c in range(6):
            pex[r * 6 + c : r * 6 + c + 1, :] = pot[16 + r : 17 + r, c * 384 : c * 384 + 384]
    pout[:, GXY : GXY + 384] = pex[...].astype(BF16)
    near = me // 6
    first = DEPTH * me - CZ * near

    def send_pot(half):
        return remote(
            pout, pin.at[half], sp.at[half], rp.at[half],
            slab=lax.rem(slab + SLAB - near - half, SLAB),
        )

    @pl.when(near != 0)
    def _():
        send_pot(0).start()

    @pl.when(near == 0)
    def _():
        pin[0] = pout[...]

    send_pot(1).start()

    tile = me // 4

    def wait1(rel, carry):
        other = peer(rel)
        remote(bt.at[0], rs1.at[other], s1.at[0], r1.at[other], band=other).wait_recv()
        return carry

    def send2(rel):
        return remote(tt.at[tile], tt.at[tile], s2.at[rel], r2.at[tile], band=peer(rel))

    def start2(rel, carry):
        send2(rel).start()
        return carry

    @pl.when(lax.rem(me, 4) == 0)
    def _():
        lax.fori_loop(1, BAND, wait1, 0)
        tt[tile] = jnp.sum(rs1[...], axis=0)
        lax.fori_loop(1, BAND, start2, 0)

    raw[NPAIR:PAD_P] = jnp.zeros((PAD_P - NPAIR, DEPTH, 2, GXY), BF16)
    fetch.wait()

    def regroup(block, carry):
        for d in range(DEPTH):
            rows = raw[pl.ds(block * 8, 8), d]
            tables[d, pl.ds(pl.multiple_of(block * 16, 16), 16), :] = rows.reshape(16, GXY)
        return carry

    lax.fori_loop(0, PAD_P // 8, regroup, 0)

    offset_row = root[...] - slab * CZ
    offset = column(offset_row)
    anchor = column(xy[...])
    species = column(kind[...])
    corner = anchor - GX * ((anchor.astype(F32) + 0.5) * (1.0 / GX)).astype(jnp.int32)
    lane = iota((ATOMS, GXY), 1)
    line = lane - GX * ((lane.astype(F32) + 0.5) * (1.0 / GX)).astype(jnp.int32)
    corner = jnp.broadcast_to(corner, (ATOMS, GXY))
    mine = jnp.broadcast_to(species, (ATOMS, ROWS)) == (iota((ATOMS, ROWS), 1) & 1)
    to_rows = jnp.where((iota((256, ROWS), 1) >> 1) == iota((256, ROWS), 0), 1.0, 0.0).astype(BF16)

    @pl.when(near != 0)
    def _():
        send_pot(0).wait_recv()

    send_pot(1).wait_recv()
    extra = []
    for half in range(2):
        packed_rows = pin[half, :, GXY : GXY + 384].astype(F32)
        for r in range(2):
            extra.append(
                jnp.concatenate([packed_rows[r * 6 + c : r * 6 + c + 1] for c in range(6)], axis=1)
            )
    extra = jnp.concatenate(extra + [jnp.zeros((12, GXY), F32)], axis=0).astype(BF16)
    planes = jnp.concatenate([pin[0, :, 0:GXY], pin[1, :, 0:GXY], extra], axis=0)
    for d in range(DEPTH):
        target = offset + (first + d)
        late = jnp.where(target >= CZ, 1, 0)
        row = target - CZ * late
        source = jnp.where(row < 16, 16 * late + row, 32 + 2 * late + row - 16)
        choose = jnp.where(
            iota((ATOMS, 48), 1) == jnp.broadcast_to(source, (ATOMS, 48)), 1.0, 0.0
        ).astype(BF16)
        turned = rotate(dot(choose, planes), anchor, True)
        turned = jnp.where(line < GX - corner, turned, pltpu.roll(turned, GX, 1))
        boxes[d] = turned.astype(BF16)

    for t in range(4):
        @pl.when(me != 4 * t)
        def _(t=t):
            remote(tt.at[t], tt.at[t], s2.at[0], r2.at[t], band=4 * t).wait_recv()

    packed = jnp.concatenate(
        [
            jnp.concatenate([tt[0], tt[1]], axis=1),
            jnp.concatenate([tt[2], tt[3]], axis=1),
        ],
        axis=0,
    ).astype(BF16)
    left = jnp.where(mine, dot(packed, to_rows), 0.0).astype(BF16)
    window = jnp.zeros((WINDOW, GXY), F32)
    for d in range(DEPTH):
        placed = rotate(dot(left, tables[d]), anchor, False)
        placed = jnp.where(line >= corner, placed, pltpu.roll(placed, GXY - GX, 1))
        onto = jnp.where(iota((WINDOW, ATOMS), 0) == offset_row + d, 1.0, 0.0).astype(BF16)
        for part in split(placed, 2):
            window = window + dot(onto, part)
    for j in range(OWNERS):
        ext[j] = window[:, j * WIDE : (j + 1) * WIDE]

    def send3(j):
        return remote(ext.at[j], rs3.at[me], s3.at[j], r3.at[me], band=8 * j // 3)

    for j in range(OWNERS):
        @pl.when(me != 8 * j // 3)
        def _(j=j):
            send3(j).start()

        @pl.when(me == 8 * j // 3)
        def _(j=j):
            rs3[me] = ext[j]

    sums = jnp.zeros((ATOMS, ROWS), F32)
    for d in range(DEPTH):
        sums = sums + dot_nt(boxes[d], tables[d])
    folded = jnp.zeros((ATOMS, 256), F32)
    for part in split(jnp.where(mine, sums, 0.0), 3):
        folded = folded + dot_nt(part, to_rows)
    for a in range(ATOMS):
        isnd[a] = folded[a : a + 1]

    def send6(rel):
        other = peer(rel)
        return remote(isnd.at[other], ircv.at[me], s6.at[rel], r6.at[me], band=other)

    def start6(rel, carry):
        send6(rel).start()
        return carry

    lax.fori_loop(1, BAND, start6, 0)
    ircv[me] = isnd[me]

    mark = (3 * me + 7) // 8
    owner = jnp.logical_and(mark < OWNERS, 8 * mark // 3 == me)
    own = jnp.minimum(mark, OWNERS - 1)

    def wait3(rel, carry):
        other = peer(rel)
        remote(ext.at[0], rs3.at[other], s3.at[0], r3.at[other], band=other).wait_recv()
        return carry

    def send4(k):
        return remote(
            st.at[k], p4.at[k - 1], s4.at[k - 1], r4.at[k - 1], slab=lax.rem(slab + k, SLAB)
        )

    def send5(rel):
        return remote(ag.at[own], ag.at[own], s5.at[rel], r5.at[own], band=peer(rel))

    def start5(rel, carry):
        send5(rel).start()
        return carry

    @pl.when(owner)
    def _():
        st[...] = jnp.zeros(st.shape, F32)
        lax.fori_loop(1, BAND, wait3, 0)
        for member in range(BAND):
            k, row = divmod(member * DEPTH, CZ)
            head = min(CZ - row, 20)
            st[k, row : row + head, :] += rs3[member, 0:head, :]
            if head < 20:
                st[k + 1, 0 : 20 - head, :] += rs3[member, head:20, :]
        for k in (1, 2, 3):
            send4(k).start()
        for k in (1, 2, 3):
            send4(k).wait_recv()
        total = st[0] + p4[0] + p4[1] + p4[2]
        exq[...] = jnp.zeros(exq.shape, F32)
        for r in range(2):
            for c in range(3):
                exq[r * 3 + c : r * 3 + c + 1, :] = total[16 + r : 17 + r, c * 128 : c * 128 + 128]
        ag[own, :, 0:WIDE] = total[0:16].astype(BF16)
        ag[own, :, WIDE : WIDE + 128] = exq[...].astype(BF16)
        lax.fori_loop(1, BAND, start5, 0)

    def wait6(rel, carry):
        other = peer(rel)
        remote(isnd.at[0], ircv.at[other], s6.at[0], r6.at[other], band=other).wait_recv()
        return carry

    lax.fori_loop(1, BAND, wait6, 0)
    ints[...] = jnp.sum(ircv[...], axis=0)[:, 0:NPAIR]

    for j in range(OWNERS):
        @pl.when(me != 8 * j // 3)
        def _(j=j):
            remote(ag.at[j], ag.at[j], s5.at[0], r5.at[j], band=8 * j // 3).wait_recv()

        dens[0:16, j * WIDE : (j + 1) * WIDE] = ag[j, :, 0:WIDE].astype(F32)
        tail = ag[j, :, WIDE : WIDE + 128].astype(F32)
        for r in range(2):
            for c in range(3):
                at = j * WIDE + c * 128
                dens[16 + r : 17 + r, at : at + 128] = tail[r * 3 + c : r * 3 + c + 1]

    for t in range(4):
        @pl.when(me != 4 * t)
        def _(t=t):
            send1(t).wait_send()

    @pl.when(near != 0)
    def _():
        send_pot(0).wait_send()

    send_pot(1).wait_send()

    def end2(rel, carry):
        send2(rel).wait_send()
        return carry

    @pl.when(lax.rem(me, 4) == 0)
    def _():
        lax.fori_loop(1, BAND, end2, 0)

    for j in range(OWNERS):
        @pl.when(me != 8 * j // 3)
        def _(j=j):
            send3(j).wait_send()

    def end6(rel, carry):
        send6(rel).wait_send()
        return carry

    lax.fori_loop(1, BAND, end6, 0)

    def end5(rel, carry):
        send5(rel).wait_send()
        return carry

    @pl.when(owner)
    def _():
        for k in (1, 2, 3):
            send4(k).wait_send()
        lax.fori_loop(1, BAND, end5, 0)


def shards(projections, occupation, augment_tables, box_root, box_xy, species, potential):
    pt = jnp.transpose(projections, (1, 2, 0)).reshape(NH * ATOMS, 256)
    tab = jnp.transpose(augment_tables, (1, 2, 0, 3))
    vmem = pl.BlockSpec(memory_space=pltpu.VMEM)
    dma = pltpu.SemaphoreType.DMA
    density, integrals = pl.pallas_call(
        kernel,
        out_shape=(
            jax.ShapeDtypeStruct((CZ, GXY), F32),
            jax.ShapeDtypeStruct((1, NPAIR), F32),
        ),
        in_specs=[vmem] * 6 + [pl.BlockSpec(memory_space=pl.ANY)],
        out_specs=(vmem, vmem),
        scratch_shapes=[
            pltpu.VMEM((PAD_P, DEPTH, 2, GXY), BF16),
            pltpu.VMEM((DEPTH, ROWS, GXY), BF16),
            pltpu.VMEM((4, 8, 128), F32),
            pltpu.VMEM((BAND, 8, 128), F32),
            pltpu.VMEM((4, 8, 128), F32),
            pltpu.VMEM((16, 384), F32),
            pltpu.VMEM((16, GXY + 384), BF16),
            pltpu.VMEM((2, 16, GXY + 384), BF16),
            pltpu.VMEM((DEPTH, ATOMS, GXY), BF16),
            pltpu.VMEM((OWNERS, WINDOW, WIDE), F32),
            pltpu.VMEM((BAND, WINDOW, WIDE), F32),
            pltpu.VMEM((4, WINDOW, WIDE), F32),
            pltpu.VMEM((3, WINDOW, WIDE), F32),
            pltpu.VMEM((16, 128), F32),
            pltpu.VMEM((OWNERS, 16, WIDE + 128), BF16),
            pltpu.VMEM((ATOMS, 1, 256), F32),
            pltpu.VMEM((BAND, 1, 256), F32),
            dma,
            dma((4,)), dma((BAND,)),
            dma((BAND,)), dma((4,)),
            dma((2,)), dma((2,)),
            dma((OWNERS,)), dma((BAND,)),
            dma((3,)), dma((3,)),
            dma((BAND,)), dma((OWNERS,)),
            dma((BAND,)), dma((BAND,)),
        ],
        compiler_params=pltpu.CompilerParams(
            collective_id=0, has_side_effects=True, vmem_limit_bytes=40 << 20
        ),
    )(
        pt,
        occupation.reshape(1, 256),
        box_root.reshape(1, ATOMS),
        box_xy.reshape(1, ATOMS),
        species.reshape(1, ATOMS),
        potential,
        tab,
    )
    return density, integrals.reshape(NPAIR, 1)


def solution(mesh):
    placed = (
        P("band", None, "slab"),
        P("band"),
        P(None, None, "band", None),
        P("slab"),
        P("slab"),
        P("slab"),
        P("slab", None),
    )
    return jax.shard_map(
        shards,
        mesh=mesh,
        in_specs=placed,
        out_specs=(P("slab", None), P(None, ("slab", "band"))),
        check_vma=False,
    )
```

```python
import jax
import jax.numpy as jnp
from jax import lax
from jax.experimental import pallas as pl
from jax.experimental.pallas import tpu as pltpu
from jax.sharding import PartitionSpec as P

GX = 48
GXY = 2304
NH = 18
NPAIR = 171
DEPTH = 3
CZ = 18
ATOMS = 16
BAND = 16
SLAB = 32
PAD_P = 176
ROWS = 2 * PAD_P
OWNERS = 6
WIDE = GXY // OWNERS
WINDOW = 24
EARLY = 6
F32 = jnp.float32
BF16 = jnp.bfloat16
NT = (((1,), (1,)), ((), ()))


def iota(shape, axis):
    return lax.broadcasted_iota(jnp.int32, shape, axis)


def dot(a, b):
    return jnp.dot(a, b, preferred_element_type=F32)


def dot_nt(a, b):
    return lax.dot_general(a, b, NT, preferred_element_type=F32)


def split(x, terms):
    parts = []
    for _ in range(terms):
        part = x.astype(BF16)
        parts.append(part)
        x = x - part.astype(F32)
    return parts


def column(row):
    picked = jnp.where(iota((ATOMS, ATOMS), 0) == iota((ATOMS, ATOMS), 1), row.astype(F32), 0.0)
    return jnp.sum(picked, axis=1, keepdims=True).astype(jnp.int32)


def rotate(values, amount, left):
    amount = jnp.broadcast_to(amount, values.shape)
    for bit in range(12):
        step = 1 << bit
        turned = pltpu.roll(values, GXY - step if left else step, 1)
        values = jnp.where((amount & step) != 0, turned, values)
    return values


def remote(src, dst, send, recv, **where):
    return pltpu.make_async_remote_copy(
        src_ref=src,
        dst_ref=dst,
        send_sem=send,
        recv_sem=recv,
        device_id=where,
        device_id_type=pl.DeviceIdType.MESH,
    )


def kernel(
    pt_hbm, occ_hbm, root_hbm, xy_hbm, kind_hbm, pot_hbm, tab, dens, ints,
    pt, occ, root, xy, kind, pot, raw, tables, bt, rs1, tt, pex, pout, pin, boxes, ext, rs3, st, p4, exq, ag, isnd, ircv,
    in_sem, tab_sem, s1, r1, s2, r2, sp, rp, s3, r3, s4, r4, s5, r5, s6, r6,
):
    me = lax.axis_index("band")
    slab = lax.axis_index("slab")

    def peer(rel):
        return lax.rem(me + rel, BAND)

    barrier = pltpu.get_barrier_semaphore()

    def greet(rel, carry):
        pl.semaphore_signal(
            barrier, inc=1, device_id={"band": peer(rel)}, device_id_type=pl.DeviceIdType.MESH
        )
        return carry

    lax.fori_loop(1, BAND, greet, 0)
    for k in (1, 2, 3, SLAB - 3, SLAB - 2, SLAB - 1):
        pl.semaphore_signal(
            barrier, inc=1, device_id={"slab": lax.rem(slab + k, SLAB)},
            device_id_type=pl.DeviceIdType.MESH,
        )
    loads = [
        pltpu.make_async_copy(src, dst, in_sem.at[n])
        for n, (src, dst) in enumerate(
            [(pt_hbm, pt), (occ_hbm, occ), (pot_hbm, pot), (root_hbm, root), (xy_hbm, xy), (kind_hbm, kind)]
        )
    ]
    for load in loads:
        load.start()
    fetch = pltpu.make_async_copy(tab, raw.at[pl.ds(0, NPAIR)], tab_sem)
    fetch.start()

    size = NH * ATOMS
    same = (iota((size, size), 0) & 15) == (iota((size, size), 1) & 15)
    pair = iota((1, 256), 1)
    i_of = jnp.zeros((1, 256), jnp.int32)
    start = jnp.zeros((1, 256), jnp.int32)
    for i in range(1, NH):
        past = pair >= i * NH - i * (i - 1) // 2
        i_of = i_of + jnp.where(past, 1, 0)
        start = start + jnp.where(past, NH - i + 1, 0)
    j_of = pair - start + i_of
    pick_j = jnp.where((iota((size, 256), 0) >> 4) == j_of, 1.0, 0.0).astype(BF16)
    loads[0].wait()
    loads[1].wait()
    p = pt[...]
    weighted = split(p.astype(F32) * occ[...], 2)
    gram = dot_nt(weighted[0], p) + dot_nt(weighted[1], p)
    spread = jnp.zeros((size, 256), F32)
    for part in split(jnp.where(same, gram, 0.0), 3):
        spread = spread + dot(part, pick_j)
    partial = jnp.zeros((ATOMS, 256), F32)
    for i in range(NH):
        partial = partial + jnp.where(i_of == i, spread[i * ATOMS : (i + 1) * ATOMS], 0.0)
    partial = partial * jnp.where(i_of == j_of, 1.0, 2.0)
    for t in range(4):
        bt[t] = partial[t // 2 * 8 : t // 2 * 8 + 8, t % 2 * 128 : t % 2 * 128 + 128]

    pl.semaphore_wait(barrier, BAND - 1 + 6)

    def send1(t):
        return remote(bt.at[t], rs1.at[me], s1.at[t], r1.at[me], band=4 * t)

    for t in range(4):
        @pl.when(me != 4 * t)
        def _(t=t):
            send1(t).start()

        @pl.when(me == 4 * t)
        def _(t=t):
            rs1[me] = bt[t]

    loads[2].wait()
    pout[:, 0:GXY] = pot[0:16, :].astype(BF16)
    pex[...] = jnp.zeros(pex.shape, F32)
    for r in range(2):
        for c in range(6):
            pex[r * 6 + c : r * 6 + c + 1, :] = pot[16 + r : 17 + r, c * 384 : c * 384 + 384]
    pout[:, GXY : GXY + 384] = pex[...].astype(BF16)
    near = me // 6
    first = DEPTH * me - CZ * near

    def send_pot(half):
        return remote(
            pout, pin.at[half], sp.at[half], rp.at[half],
            slab=lax.rem(slab + SLAB - near - half, SLAB),
        )

    @pl.when(near != 0)
    def _():
        send_pot(0).start()

    @pl.when(near == 0)
    def _():
        pin[0] = pout[...]

    send_pot(1).start()

    raw[NPAIR:PAD_P] = jnp.zeros((PAD_P - NPAIR, DEPTH, 2, GXY), BF16)
    fetch.wait()

    def regroup(block, carry):
        for d in range(DEPTH):
            rows = raw[pl.ds(block * 8, 8), d]
            tables[d, pl.ds(pl.multiple_of(block * 16, 16), 16), :] = rows.reshape(16, GXY)
        return carry

    lax.fori_loop(0, EARLY, regroup, 0)

    tile = me // 4

    def wait1(rel, carry):
        other = peer(rel)
        remote(bt.at[0], rs1.at[other], s1.at[0], r1.at[other], band=other).wait_recv()
        return carry

    def send2(rel):
        return remote(tt.at[tile], tt.at[tile], s2.at[rel], r2.at[tile], band=peer(rel))

    def start2(rel, carry):
        send2(rel).start()
        return carry

    @pl.when(lax.rem(me, 4) == 0)
    def _():
        lax.fori_loop(1, BAND, wait1, 0)
        tt[tile] = jnp.sum(rs1[...], axis=0)
        lax.fori_loop(1, BAND, start2, 0)

    lax.fori_loop(EARLY, PAD_P // 8, regroup, 0)
    for load in loads[3:]:
        load.wait()

    offset_row = root[...] - slab * CZ
    offset = column(offset_row)
    anchor = column(xy[...])
    species = column(kind[...])
    corner = anchor - GX * ((anchor.astype(F32) + 0.5) * (1.0 / GX)).astype(jnp.int32)
    lane = iota((ATOMS, GXY), 1)
    line = lane - GX * ((lane.astype(F32) + 0.5) * (1.0 / GX)).astype(jnp.int32)
    corner = jnp.broadcast_to(corner, (ATOMS, GXY))
    mine = jnp.broadcast_to(species, (ATOMS, ROWS)) == (iota((ATOMS, ROWS), 1) & 1)
    to_rows = jnp.where((iota((256, ROWS), 1) >> 1) == iota((256, ROWS), 0), 1.0, 0.0).astype(BF16)

    for t in range(4):
        @pl.when(me != 4 * t)
        def _(t=t):
            remote(tt.at[t], tt.at[t], s2.at[0], r2.at[t], band=4 * t).wait_recv()

    packed = jnp.concatenate(
        [
            jnp.concatenate([tt[0], tt[1]], axis=1),
            jnp.concatenate([tt[2], tt[3]], axis=1),
        ],
        axis=0,
    ).astype(BF16)
    left = jnp.where(mine, dot(packed, to_rows), 0.0).astype(BF16)
    window = jnp.zeros((WINDOW, GXY), F32)
    for d in range(DEPTH):
        placed = rotate(dot(left, tables[d]), anchor, False)
        placed = jnp.where(line >= corner, placed, pltpu.roll(placed, GXY - GX, 1))
        onto = jnp.where(iota((WINDOW, ATOMS), 0) == offset_row + d, 1.0, 0.0).astype(BF16)
        for part in split(placed, 2):
            window = window + dot(onto, part)
    for j in range(OWNERS):
        ext[j] = window[:, j * WIDE : (j + 1) * WIDE]

    def send3(j):
        return remote(ext.at[j], rs3.at[me], s3.at[j], r3.at[me], band=8 * j // 3)

    for j in range(OWNERS):
        @pl.when(me != 8 * j // 3)
        def _(j=j):
            send3(j).start()

        @pl.when(me == 8 * j // 3)
        def _(j=j):
            rs3[me] = ext[j]

    @pl.when(near != 0)
    def _():
        send_pot(0).wait_recv()

    send_pot(1).wait_recv()
    extra = []
    for half in range(2):
        packed_rows = pin[half, :, GXY : GXY + 384].astype(F32)
        for r in range(2):
            extra.append(
                jnp.concatenate([packed_rows[r * 6 + c : r * 6 + c + 1] for c in range(6)], axis=1)
            )
    extra = jnp.concatenate(extra + [jnp.zeros((12, GXY), F32)], axis=0).astype(BF16)
    planes = jnp.concatenate([pin[0, :, 0:GXY], pin[1, :, 0:GXY], extra], axis=0)
    for d in range(DEPTH):
        target = offset + (first + d)
        late = jnp.where(target >= CZ, 1, 0)
        row = target - CZ * late
        source = jnp.where(row < 16, 16 * late + row, 32 + 2 * late + row - 16)
        choose = jnp.where(
            iota((ATOMS, 48), 1) == jnp.broadcast_to(source, (ATOMS, 48)), 1.0, 0.0
        ).astype(BF16)
        turned = rotate(dot(choose, planes), anchor, True)
        turned = jnp.where(line < GX - corner, turned, pltpu.roll(turned, GX, 1))
        boxes[d] = turned.astype(BF16)

    sums = jnp.zeros((ATOMS, ROWS), F32)
    for d in range(DEPTH):
        sums = sums + dot_nt(boxes[d], tables[d])
    folded = jnp.zeros((ATOMS, 256), F32)
    for part in split(jnp.where(mine, sums, 0.0), 3):
        folded = folded + dot_nt(part, to_rows)
    for a in range(ATOMS):
        isnd[a] = folded[a : a + 1]

    def send6(rel):
        other = peer(rel)
        return remote(isnd.at[other], ircv.at[me], s6.at[rel], r6.at[me], band=other)

    def start6(rel, carry):
        send6(rel).start()
        return carry

    lax.fori_loop(1, BAND, start6, 0)
    ircv[me] = isnd[me]

    mark = (3 * me + 7) // 8
    owner = jnp.logical_and(mark < OWNERS, 8 * mark // 3 == me)
    own = jnp.minimum(mark, OWNERS - 1)

    def wait3(rel, carry):
        other = peer(rel)
        remote(ext.at[0], rs3.at[other], s3.at[0], r3.at[other], band=other).wait_recv()
        return carry

    def send4(k):
        return remote(
            st.at[k], p4.at[k - 1], s4.at[k - 1], r4.at[k - 1], slab=lax.rem(slab + k, SLAB)
        )

    def send5(rel):
        return remote(ag.at[own], ag.at[own], s5.at[rel], r5.at[own], band=peer(rel))

    def start5(rel, carry):
        send5(rel).start()
        return carry

    @pl.when(owner)
    def _():
        st[...] = jnp.zeros(st.shape, F32)
        lax.fori_loop(1, BAND, wait3, 0)
        for member in range(BAND):
            k, row = divmod(member * DEPTH, CZ)
            head = min(CZ - row, 20)
            st[k, row : row + head, :] += rs3[member, 0:head, :]
            if head < 20:
                st[k + 1, 0 : 20 - head, :] += rs3[member, head:20, :]
        for k in (1, 2, 3):
            send4(k).start()
        for k in (1, 2, 3):
            send4(k).wait_recv()
        total = st[0] + p4[0] + p4[1] + p4[2]
        exq[...] = jnp.zeros(exq.shape, F32)
        for r in range(2):
            for c in range(3):
                exq[r * 3 + c : r * 3 + c + 1, :] = total[16 + r : 17 + r, c * 128 : c * 128 + 128]
        ag[own, :, 0:WIDE] = total[0:16].astype(BF16)
        ag[own, :, WIDE : WIDE + 128] = exq[...].astype(BF16)
        lax.fori_loop(1, BAND, start5, 0)

    def wait6(rel, carry):
        other = peer(rel)
        remote(isnd.at[0], ircv.at[other], s6.at[0], r6.at[other], band=other).wait_recv()
        return carry

    lax.fori_loop(1, BAND, wait6, 0)
    ints[...] = jnp.sum(ircv[...], axis=0)[:, 0:NPAIR]

    for j in range(OWNERS):
        @pl.when(me != 8 * j // 3)
        def _(j=j):
            remote(ag.at[j], ag.at[j], s5.at[0], r5.at[j], band=8 * j // 3).wait_recv()

        dens[0:16, j * WIDE : (j + 1) * WIDE] = ag[j, :, 0:WIDE].astype(F32)
        tail = ag[j, :, WIDE : WIDE + 128].astype(F32)
        for r in range(2):
            for c in range(3):
                at = j * WIDE + c * 128
                dens[16 + r : 17 + r, at : at + 128] = tail[r * 3 + c : r * 3 + c + 1]

    for t in range(4):
        @pl.when(me != 4 * t)
        def _(t=t):
            send1(t).wait_send()

    @pl.when(near != 0)
    def _():
        send_pot(0).wait_send()

    send_pot(1).wait_send()

    def end2(rel, carry):
        send2(rel).wait_send()
        return carry

    @pl.when(lax.rem(me, 4) == 0)
    def _():
        lax.fori_loop(1, BAND, end2, 0)

    for j in range(OWNERS):
        @pl.when(me != 8 * j // 3)
        def _(j=j):
            send3(j).wait_send()

    def end6(rel, carry):
        send6(rel).wait_send()
        return carry

    lax.fori_loop(1, BAND, end6, 0)

    def end5(rel, carry):
        send5(rel).wait_send()
        return carry

    @pl.when(owner)
    def _():
        for k in (1, 2, 3):
            send4(k).wait_send()
        lax.fori_loop(1, BAND, end5, 0)


def shards(projections, occupation, augment_tables, box_root, box_xy, species, potential):
    pt = jnp.transpose(projections, (1, 2, 0)).reshape(NH * ATOMS, 256)
    tab = jnp.transpose(augment_tables, (1, 2, 0, 3))
    vmem = pl.BlockSpec(memory_space=pltpu.VMEM)
    dma = pltpu.SemaphoreType.DMA
    density, integrals = pl.pallas_call(
        kernel,
        out_shape=(
            jax.ShapeDtypeStruct((CZ, GXY), F32),
            jax.ShapeDtypeStruct((1, NPAIR), F32),
        ),
        in_specs=[pl.BlockSpec(memory_space=pltpu.HBM)] * 7,
        out_specs=(vmem, vmem),
        scratch_shapes=[
            pltpu.VMEM((NH * ATOMS, 256), BF16),
            pltpu.VMEM((1, 256), F32),
            pltpu.VMEM((1, ATOMS), jnp.int32),
            pltpu.VMEM((1, ATOMS), jnp.int32),
            pltpu.VMEM((1, ATOMS), jnp.int32),
            pltpu.VMEM((CZ, GXY), F32),
            pltpu.VMEM((PAD_P, DEPTH, 2, GXY), BF16),
            pltpu.VMEM((DEPTH, ROWS, GXY), BF16),
            pltpu.VMEM((4, 8, 128), F32),
            pltpu.VMEM((BAND, 8, 128), F32),
            pltpu.VMEM((4, 8, 128), F32),
            pltpu.VMEM((16, 384), F32),
            pltpu.VMEM((16, GXY + 384), BF16),
            pltpu.VMEM((2, 16, GXY + 384), BF16),
            pltpu.VMEM((DEPTH, ATOMS, GXY), BF16),
            pltpu.VMEM((OWNERS, WINDOW, WIDE), F32),
            pltpu.VMEM((BAND, WINDOW, WIDE), F32),
            pltpu.VMEM((4, WINDOW, WIDE), F32),
            pltpu.VMEM((3, WINDOW, WIDE), F32),
            pltpu.VMEM((16, 128), F32),
            pltpu.VMEM((OWNERS, 16, WIDE + 128), BF16),
            pltpu.VMEM((ATOMS, 1, 256), F32),
            pltpu.VMEM((BAND, 1, 256), F32),
            dma((6,)),
            dma,
            dma((4,)), dma((BAND,)),
            dma((BAND,)), dma((4,)),
            dma((2,)), dma((2,)),
            dma((OWNERS,)), dma((BAND,)),
            dma((3,)), dma((3,)),
            dma((BAND,)), dma((OWNERS,)),
            dma((BAND,)), dma((BAND,)),
        ],
        compiler_params=pltpu.CompilerParams(
            collective_id=0, has_side_effects=True, vmem_limit_bytes=56 << 20
        ),
    )(
        pt,
        occupation.reshape(1, 256),
        box_root.reshape(1, ATOMS),
        box_xy.reshape(1, ATOMS),
        species.reshape(1, ATOMS),
        potential,
        tab,
    )
    return density, integrals.reshape(NPAIR, 1)


def solution(mesh):
    placed = (
        P("band", None, "slab"),
        P("band"),
        P(None, None, "band", None),
        P("slab"),
        P("slab"),
        P("slab"),
        P("slab", None),
    )
    return jax.shard_map(
        shards,
        mesh=mesh,
        in_specs=placed,
        out_specs=(P("slab", None), P(None, ("slab", "band"))),
        check_vma=False,
    )
```

```python
import jax
import jax.numpy as jnp
from jax import lax
from jax.experimental import pallas as pl
from jax.experimental.pallas import tpu as pltpu
from jax.sharding import PartitionSpec as P

GX = 48
GXY = 2304
NH = 18
NPAIR = 171
DEPTH = 3
CZ = 18
ATOMS = 16
BAND = 16
SLAB = 32
PAD_P = 176
ROWS = 2 * PAD_P
OWNERS = 6
WIDE = GXY // OWNERS
WINDOW = 24
TILES = 18
F32 = jnp.float32
BF16 = jnp.bfloat16
NT = (((1,), (1,)), ((), ()))


def iota(shape, axis):
    return lax.broadcasted_iota(jnp.int32, shape, axis)


def dot(a, b):
    return jnp.dot(a, b, preferred_element_type=F32)


def dot_nt(a, b):
    return lax.dot_general(a, b, NT, preferred_element_type=F32)


def split(x, terms):
    parts = []
    for _ in range(terms):
        part = x.astype(BF16)
        parts.append(part)
        x = x - part.astype(F32)
    return parts


def column(row):
    picked = jnp.where(iota((ATOMS, ATOMS), 0) == iota((ATOMS, ATOMS), 1), row.astype(F32), 0.0)
    return jnp.sum(picked, axis=1, keepdims=True).astype(jnp.int32)


def rows_of(tables, d, c):
    return jnp.concatenate(
        [tables[d, 2 * c].reshape(ROWS, 128), tables[d, 2 * c + 1].reshape(ROWS, 128)], axis=1
    )


def take(sem, landed):
    pltpu.make_async_copy(landed, landed, sem).wait()


def rotate(values, amount, left):
    amount = jnp.broadcast_to(amount, values.shape)
    for bit in range(12):
        step = 1 << bit
        turned = pltpu.roll(values, GXY - step if left else step, 1)
        values = jnp.where((amount & step) != 0, turned, values)
    return values


def remote(src, dst, send, recv, **where):
    return pltpu.make_async_remote_copy(
        src_ref=src,
        dst_ref=dst,
        send_sem=send,
        recv_sem=recv,
        device_id=where,
        device_id_type=pl.DeviceIdType.MESH,
    )


def kernel(
    pt_hbm, occ_hbm, root_hbm, xy_hbm, kind_hbm, pot_hbm, tab, dens, ints,
    pt, occ, root, xy, kind, pot, tables, bt, rs1, tt, pex, pout, pin, boxes, ext, rs3, st, p4, exq, ag, isnd, ircv,
    in_sem, tab_sem, s1, r1, s2, r2, sp, rp, s3, r3, s4, r4, s5, r5, s6, r6,
):
    me = lax.axis_index("band")
    slab = lax.axis_index("slab")

    def peer(rel):
        return lax.rem(me + rel, BAND)

    barrier = pltpu.get_barrier_semaphore()

    def greet(rel, carry):
        pl.semaphore_signal(
            barrier, inc=1, device_id={"band": peer(rel)}, device_id_type=pl.DeviceIdType.MESH
        )
        return carry

    lax.fori_loop(1, BAND, greet, 0)
    for k in (1, 2, 3, SLAB - 3, SLAB - 2, SLAB - 1):
        pl.semaphore_signal(
            barrier, inc=1, device_id={"slab": lax.rem(slab + k, SLAB)},
            device_id_type=pl.DeviceIdType.MESH,
        )
    loads = [
        pltpu.make_async_copy(src, dst, in_sem.at[n])
        for n, (src, dst) in enumerate(
            [(pt_hbm, pt), (occ_hbm, occ), (pot_hbm, pot), (root_hbm, root), (xy_hbm, xy), (kind_hbm, kind)]
        )
    ]
    for load in loads:
        load.start()
    tables[:, :, NPAIR:PAD_P] = jnp.zeros((DEPTH, TILES, PAD_P - NPAIR, 2, 128), BF16)
    for d in range(DEPTH):
        for c in range(TILES):
            pltpu.make_async_copy(
                tab.at[:, d, c], tables.at[d, c, pl.ds(0, NPAIR)], tab_sem.at[d]
            ).start()

    size = NH * ATOMS
    same = (iota((size, size), 0) & 15) == (iota((size, size), 1) & 15)
    pair = iota((1, 256), 1)
    i_of = jnp.zeros((1, 256), jnp.int32)
    start = jnp.zeros((1, 256), jnp.int32)
    for i in range(1, NH):
        past = pair >= i * NH - i * (i - 1) // 2
        i_of = i_of + jnp.where(past, 1, 0)
        start = start + jnp.where(past, NH - i + 1, 0)
    j_of = pair - start + i_of
    pick_j = jnp.where((iota((size, 256), 0) >> 4) == j_of, 1.0, 0.0).astype(BF16)
    loads[0].wait()
    loads[1].wait()
    p = pt[...]
    weighted = split(p.astype(F32) * occ[...], 2)
    gram = dot_nt(weighted[0], p) + dot_nt(weighted[1], p)
    spread = jnp.zeros((size, 256), F32)
    for part in split(jnp.where(same, gram, 0.0), 3):
        spread = spread + dot(part, pick_j)
    partial = jnp.zeros((ATOMS, 256), F32)
    for i in range(NH):
        partial = partial + jnp.where(i_of == i, spread[i * ATOMS : (i + 1) * ATOMS], 0.0)
    partial = partial * jnp.where(i_of == j_of, 1.0, 2.0)
    for t in range(4):
        bt[t] = partial[t // 2 * 8 : t // 2 * 8 + 8, t % 2 * 128 : t % 2 * 128 + 128]

    pl.semaphore_wait(barrier, BAND - 1 + 6)

    def send1(t):
        return remote(bt.at[t], rs1.at[me], s1.at[t], r1.at[0], band=4 * t)

    for t in range(4):
        @pl.when(me != 4 * t)
        def _(t=t):
            send1(t).start()

        @pl.when(me == 4 * t)
        def _(t=t):
            rs1[me] = bt[t]

    loads[2].wait()
    pout[:, 0:GXY] = pot[0:16, :].astype(BF16)
    pex[...] = jnp.zeros(pex.shape, F32)
    for r in range(2):
        for c in range(6):
            pex[r * 6 + c : r * 6 + c + 1, :] = pot[16 + r : 17 + r, c * 384 : c * 384 + 384]
    pout[:, GXY : GXY + 384] = pex[...].astype(BF16)
    near = me // 6
    first = DEPTH * me - CZ * near

    def send_pot(half):
        return remote(
            pout, pin.at[half], sp.at[half], rp.at[half],
            slab=lax.rem(slab + SLAB - near - half, SLAB),
        )

    @pl.when(near != 0)
    def _():
        send_pot(0).start()

    @pl.when(near == 0)
    def _():
        pin[0] = pout[...]

    send_pot(1).start()

    tile = me // 4

    def send2(rel):
        return remote(tt.at[tile], tt.at[tile], s2.at[0], r2.at[tile], band=peer(rel))

    def start2(rel, carry):
        send2(rel).start()
        return carry

    @pl.when(lax.rem(me, 4) == 0)
    def _():
        take(r1.at[0], rs1.at[pl.ds(0, BAND - 1)])
        tt[tile] = jnp.sum(rs1[...], axis=0)
        lax.fori_loop(1, BAND, start2, 0)

    for d in range(DEPTH):
        part = tables.at[d, :, pl.ds(0, NPAIR)]
        pltpu.make_async_copy(part, part, tab_sem.at[d]).wait()
    for load in loads[3:]:
        load.wait()

    offset_row = root[...] - slab * CZ
    offset = column(offset_row)
    anchor = column(xy[...])
    species = column(kind[...])
    corner = anchor - GX * ((anchor.astype(F32) + 0.5) * (1.0 / GX)).astype(jnp.int32)
    lane = iota((ATOMS, GXY), 1)
    line = lane - GX * ((lane.astype(F32) + 0.5) * (1.0 / GX)).astype(jnp.int32)
    corner = jnp.broadcast_to(corner, (ATOMS, GXY))
    mine = jnp.broadcast_to(species, (ATOMS, ROWS)) == (iota((ATOMS, ROWS), 1) & 1)
    to_rows = jnp.where((iota((256, ROWS), 1) >> 1) == iota((256, ROWS), 0), 1.0, 0.0).astype(BF16)

    for t in range(4):
        @pl.when(me != 4 * t)
        def _(t=t):
            remote(tt.at[t], tt.at[t], s2.at[0], r2.at[t], band=4 * t).wait_recv()

    packed = jnp.concatenate(
        [
            jnp.concatenate([tt[0], tt[1]], axis=1),
            jnp.concatenate([tt[2], tt[3]], axis=1),
        ],
        axis=0,
    ).astype(BF16)
    left = jnp.where(mine, dot(packed, to_rows), 0.0).astype(BF16)
    window = jnp.zeros((WINDOW, GXY), F32)
    for d in range(DEPTH):
        terms = [dot(left, rows_of(tables, d, c)) for c in range(TILES // 2)]
        placed = rotate(jnp.concatenate(terms, axis=1), anchor, False)
        placed = jnp.where(line >= corner, placed, pltpu.roll(placed, GXY - GX, 1))
        onto = jnp.where(iota((WINDOW, ATOMS), 0) == offset_row + d, 1.0, 0.0).astype(BF16)
        for part in split(placed, 2):
            window = window + dot(onto, part)
    for j in range(OWNERS):
        ext[j, :, 0:WIDE] = window[0:16, j * WIDE : (j + 1) * WIDE].astype(BF16)
        ends = [window[16:24, j * WIDE + c * 128 : j * WIDE + c * 128 + 128] for c in range(3)]
        ends = jnp.concatenate([ends[0] + pltpu.roll(ends[1], 4, 0), ends[2]], axis=0)
        ext[j, :, WIDE : WIDE + 128] = ends.astype(BF16)

    def send3(j):
        return remote(ext.at[j], rs3.at[me], s3.at[j], r3.at[0], band=8 * j // 3)

    for j in range(OWNERS):
        @pl.when(me != 8 * j // 3)
        def _(j=j):
            send3(j).start()

        @pl.when(me == 8 * j // 3)
        def _(j=j):
            rs3[me] = ext[j]

    @pl.when(near != 0)
    def _():
        send_pot(0).wait_recv()

    send_pot(1).wait_recv()
    extra = []
    for half in range(2):
        packed_rows = pin[half, :, GXY : GXY + 384].astype(F32)
        for r in range(2):
            extra.append(
                jnp.concatenate([packed_rows[r * 6 + c : r * 6 + c + 1] for c in range(6)], axis=1)
            )
    extra = jnp.concatenate(extra + [jnp.zeros((12, GXY), F32)], axis=0).astype(BF16)
    planes = jnp.concatenate([pin[0, :, 0:GXY], pin[1, :, 0:GXY], extra], axis=0)
    for d in range(DEPTH):
        target = offset + (first + d)
        late = jnp.where(target >= CZ, 1, 0)
        row = target - CZ * late
        source = jnp.where(row < 16, 16 * late + row, 32 + 2 * late + row - 16)
        choose = jnp.where(
            iota((ATOMS, 48), 1) == jnp.broadcast_to(source, (ATOMS, 48)), 1.0, 0.0
        ).astype(BF16)
        turned = rotate(dot(choose, planes), anchor, True)
        turned = jnp.where(line < GX - corner, turned, pltpu.roll(turned, GX, 1))
        boxes[d] = turned.astype(BF16)

    mark = (3 * me + 7) // 8
    owner = jnp.logical_and(mark < OWNERS, 8 * mark // 3 == me)
    own = jnp.minimum(mark, OWNERS - 1)

    def send4(k):
        return remote(
            st.at[k], p4.at[k - 1], s4.at[k - 1], r4.at[k - 1], slab=lax.rem(slab + k, SLAB)
        )

    def send5(rel):
        return remote(ag.at[own], ag.at[own], s5.at[0], r5.at[own], band=peer(rel))

    def start5(rel, carry):
        send5(rel).start()
        return carry

    @pl.when(owner)
    def _():
        out_row = iota((4 * WINDOW, 256), 0)
        block = jnp.zeros(out_row.shape, jnp.int32)
        for k in (1, 2, 3):
            block = block + jnp.where(out_row >= k * WINDOW, 1, 0)
        out_row = out_row - WINDOW * block
        plane = jnp.where(out_row < CZ, out_row + CZ * block, -1)
        source = iota((4 * WINDOW, 256), 1)
        base = DEPTH * (source >> 4)
        source = source & 15
        gather = jnp.where(plane == base + source, 1.0, 0.0).astype(BF16)
        tails = [
            jnp.where(
                jnp.logical_and(source >> 2 == c, plane == base + 16 + (source & 3)), 1.0, 0.0
            ).astype(BF16)
            for c in range(3)
        ]
        take(r3.at[0], rs3.at[pl.ds(0, BAND - 1)])
        end = rs3[:, :, WIDE : WIDE + 128].reshape(256, 128)
        whole = dot(gather, rs3[:, :, 0:WIDE].reshape(256, WIDE))
        whole = whole + jnp.concatenate([dot(tails[c], end) for c in range(3)], axis=1)
        for k in range(4):
            st[k] = whole[k * WINDOW : (k + 1) * WINDOW]
        for k in (1, 2, 3):
            send4(k).start()

    sums = jnp.zeros((ATOMS, ROWS), F32)
    for d in range(DEPTH):
        for c in range(TILES // 2):
            sums = sums + dot_nt(boxes[d, :, 256 * c : 256 * c + 256], rows_of(tables, d, c))
    folded = jnp.zeros((ATOMS, 256), F32)
    for part in split(jnp.where(mine, sums, 0.0), 3):
        folded = folded + dot_nt(part, to_rows)
    for a in range(ATOMS):
        isnd[a] = folded[a : a + 1]

    def send6(rel):
        other = peer(rel)
        return remote(isnd.at[other], ircv.at[me], s6.at[0], r6.at[0], band=other)

    def start6(rel, carry):
        send6(rel).start()
        return carry

    lax.fori_loop(1, BAND, start6, 0)
    ircv[me] = isnd[me]

    @pl.when(owner)
    def _():
        for k in (1, 2, 3):
            send4(k).wait_recv()
        total = st[0] + p4[0] + p4[1] + p4[2]
        exq[...] = jnp.zeros(exq.shape, F32)
        for r in range(2):
            for c in range(3):
                exq[r * 3 + c : r * 3 + c + 1, :] = total[16 + r : 17 + r, c * 128 : c * 128 + 128]
        ag[own, :, 0:WIDE] = total[0:16].astype(BF16)
        ag[own, :, WIDE : WIDE + 128] = exq[...].astype(BF16)
        lax.fori_loop(1, BAND, start5, 0)

    take(r6.at[0], ircv.at[pl.ds(0, BAND - 1)])
    ints[...] = jnp.sum(ircv[...], axis=0)[:, 0:NPAIR]

    for j in range(OWNERS):
        @pl.when(me != 8 * j // 3)
        def _(j=j):
            remote(ag.at[j], ag.at[j], s5.at[0], r5.at[j], band=8 * j // 3).wait_recv()

        dens[0:16, j * WIDE : (j + 1) * WIDE] = ag[j, :, 0:WIDE].astype(F32)
        tail = ag[j, :, WIDE : WIDE + 128].astype(F32)
        for r in range(2):
            for c in range(3):
                at = j * WIDE + c * 128
                dens[16 + r : 17 + r, at : at + 128] = tail[r * 3 + c : r * 3 + c + 1]

    for t in range(4):
        @pl.when(me != 4 * t)
        def _(t=t):
            send1(t).wait_send()

    @pl.when(near != 0)
    def _():
        send_pot(0).wait_send()

    send_pot(1).wait_send()

    @pl.when(lax.rem(me, 4) == 0)
    def _():
        take(s2.at[0], rs1.at[pl.ds(0, BAND - 1)])

    for j in range(OWNERS):
        @pl.when(me != 8 * j // 3)
        def _(j=j):
            send3(j).wait_send()

    take(s6.at[0], ircv.at[pl.ds(0, BAND - 1)])

    @pl.when(owner)
    def _():
        for k in (1, 2, 3):
            send4(k).wait_send()
        take(s5.at[0], rs3.at[pl.ds(0, BAND - 1)])


def shards(projections, occupation, augment_tables, box_root, box_xy, species, potential):
    pt = jnp.transpose(projections, (1, 2, 0)).reshape(NH * ATOMS, 256)
    tab = jnp.transpose(augment_tables.reshape(2, NPAIR, DEPTH, TILES, 128), (1, 2, 3, 0, 4))
    vmem = pl.BlockSpec(memory_space=pltpu.VMEM)
    dma = pltpu.SemaphoreType.DMA
    density, integrals = pl.pallas_call(
        kernel,
        out_shape=(
            jax.ShapeDtypeStruct((CZ, GXY), F32),
            jax.ShapeDtypeStruct((1, NPAIR), F32),
        ),
        in_specs=[pl.BlockSpec(memory_space=pltpu.HBM)] * 7,
        out_specs=(vmem, vmem),
        scratch_shapes=[
            pltpu.VMEM((NH * ATOMS, 256), BF16),
            pltpu.VMEM((1, 256), F32),
            pltpu.VMEM((1, ATOMS), jnp.int32),
            pltpu.VMEM((1, ATOMS), jnp.int32),
            pltpu.VMEM((1, ATOMS), jnp.int32),
            pltpu.VMEM((CZ, GXY), F32),
            pltpu.VMEM((DEPTH, TILES, PAD_P, 2, 128), BF16),
            pltpu.VMEM((4, 8, 128), F32),
            pltpu.VMEM((BAND, 8, 128), F32),
            pltpu.VMEM((4, 8, 128), F32),
            pltpu.VMEM((16, 384), F32),
            pltpu.VMEM((16, GXY + 384), BF16),
            pltpu.VMEM((2, 16, GXY + 384), BF16),
            pltpu.VMEM((DEPTH, ATOMS, GXY), BF16),
            pltpu.VMEM((OWNERS, 16, WIDE + 128), BF16),
            pltpu.VMEM((BAND, 16, WIDE + 128), BF16),
            pltpu.VMEM((4, WINDOW, WIDE), F32),
            pltpu.VMEM((3, WINDOW, WIDE), F32),
            pltpu.VMEM((16, 128), F32),
            pltpu.VMEM((OWNERS, 16, WIDE + 128), BF16),
            pltpu.VMEM((ATOMS, 1, 256), F32),
            pltpu.VMEM((BAND, 1, 256), F32),
            dma((6,)),
            dma((DEPTH,)),
            dma((4,)), dma((1,)),
            dma((1,)), dma((4,)),
            dma((2,)), dma((2,)),
            dma((OWNERS,)), dma((1,)),
            dma((3,)), dma((3,)),
            dma((1,)), dma((OWNERS,)),
            dma((1,)), dma((1,)),
        ],
        compiler_params=pltpu.CompilerParams(
            collective_id=0, has_side_effects=True, vmem_limit_bytes=56 << 20
        ),
    )(
        pt,
        occupation.reshape(1, 256),
        box_root.reshape(1, ATOMS),
        box_xy.reshape(1, ATOMS),
        species.reshape(1, ATOMS),
        potential,
        tab,
    )
    return density, integrals.reshape(NPAIR, 1)


def solution(mesh):
    placed = (
        P("band", None, "slab"),
        P("band"),
        P(None, None, "band", None),
        P("slab"),
        P("slab"),
        P("slab"),
        P("slab", None),
    )
    return jax.shard_map(
        shards,
        mesh=mesh,
        in_specs=placed,
        out_specs=(P("slab", None), P(None, ("slab", "band"))),
        check_vma=False,
    )
```

```python
import jax
import jax.numpy as jnp
from jax import lax
from jax.experimental import pallas as pl
from jax.experimental.pallas import tpu as pltpu
from jax.sharding import PartitionSpec as P

GX = 48
GXY = 2304
NH = 18
NPAIR = 171
DEPTH = 3
CZ = 18
ATOMS = 16
BAND = 16
SLAB = 32
PAD_P = 176
ROWS = 2 * PAD_P
OWNERS = 6
WIDE = GXY // OWNERS
WINDOW = 24
TILES = 18
F32 = jnp.float32
BF16 = jnp.bfloat16
NT = (((1,), (1,)), ((), ()))


def iota(shape, axis):
    return lax.broadcasted_iota(jnp.int32, shape, axis)


def dot(a, b):
    return jnp.dot(a, b, preferred_element_type=F32)


def dot_nt(a, b):
    return lax.dot_general(a, b, NT, preferred_element_type=F32)


def split(x, terms):
    parts = []
    for _ in range(terms):
        part = x.astype(BF16)
        parts.append(part)
        x = x - part.astype(F32)
    return parts


def column(row):
    picked = jnp.where(iota((ATOMS, ATOMS), 0) == iota((ATOMS, ATOMS), 1), row.astype(F32), 0.0)
    return jnp.sum(picked, axis=1, keepdims=True).astype(jnp.int32)


def rows_of(tables, d, c):
    return jnp.concatenate(
        [tables[d, 2 * c].reshape(ROWS, 128), tables[d, 2 * c + 1].reshape(ROWS, 128)], axis=1
    )


def take(sem, landed):
    pltpu.make_async_copy(landed, landed, sem).wait()


def rotate(values, anchors, corners, left):
    lane = iota((8, 128), 1)

    def turn(v, step):
        back = GXY - step if left else step
        back = back % 128
        turned = [pltpu.roll(x, back, 1) for x in v]
        if left:
            return [jnp.where(lane < back, turned[c], turned[(c + 1) % TILES]) for c in range(TILES)]
        return [jnp.where(lane >= back, turned[c], turned[c - 1]) for c in range(TILES)]

    def eight_rows(i, carry):
        rows = pl.ds(pl.multiple_of(8 * i, 8), 8)
        amount = anchors[rows, :]
        v = [values[rows, 128 * c : 128 * c + 128] for c in range(TILES)]
        for bit in range(12):
            on = (amount & (1 << bit)) != 0
            if bit < 7:
                moved = turn(v, 1 << bit)
            else:
                hop = 1 << (bit - 7)
                moved = [v[(c + hop if left else c - hop) % TILES] for c in range(TILES)]
            v = [jnp.where(on, moved[c], v[c]) for c in range(TILES)]
        corner = corners[rows, :]
        inside = []
        for c in range(3):
            line = lane + 128 * c % GX
            for end in (GX, 2 * GX, 3 * GX):
                line = line - jnp.where(lane + 128 * c % GX >= end, GX, 0)
            inside.append(line < GX - corner if left else line >= corner)
        wrap = [pltpu.roll(x, GX if left else 128 - GX, 1) for x in v]
        for c in range(TILES):
            if left:
                wrapped = jnp.where(lane >= GX, wrap[c], wrap[c - 1])
            else:
                wrapped = jnp.where(lane < 128 - GX, wrap[c], wrap[(c + 1) % TILES])
            values[rows, 128 * c : 128 * c + 128] = jnp.where(inside[c % 3], v[c], wrapped)
        return carry

    lax.fori_loop(0, DEPTH * ATOMS // 8, eight_rows, 0)


def remote(src, dst, send, recv, **where):
    return pltpu.make_async_remote_copy(
        src_ref=src,
        dst_ref=dst,
        send_sem=send,
        recv_sem=recv,
        device_id=where,
        device_id_type=pl.DeviceIdType.MESH,
    )


def kernel(
    pt_hbm, occ_hbm, root_hbm, xy_hbm, kind_hbm, pot_hbm, tab, dens, ints,
    pt, occ, root, xy, kind, pot, tables, bt, rs1, tt, pex, pout, pin, boxes, ext, rs3, st, p4, values, anchors, corners, ag, isnd, ircv,
    in_sem, tab_sem, s1, r1, s2, r2, sp, rp, s3, r3, s4, r4, s5, r5, s6, r6,
):
    me = lax.axis_index("band")
    slab = lax.axis_index("slab")

    def peer(rel):
        return lax.rem(me + rel, BAND)

    loads = [
        pltpu.make_async_copy(src, dst, in_sem.at[n])
        for n, (src, dst) in enumerate(
            [(pt_hbm, pt), (occ_hbm, occ), (pot_hbm, pot), (root_hbm, root), (xy_hbm, xy), (kind_hbm, kind)]
        )
    ]
    loads[0].start()
    loads[1].start()
    barrier = pltpu.get_barrier_semaphore()

    def greet(rel, carry):
        pl.semaphore_signal(
            barrier, inc=1, device_id={"band": peer(rel)}, device_id_type=pl.DeviceIdType.MESH
        )
        return carry

    lax.fori_loop(1, BAND, greet, 0)
    for k in (1, 2, 3, SLAB - 3, SLAB - 2, SLAB - 1):
        pl.semaphore_signal(
            barrier, inc=1, device_id={"slab": lax.rem(slab + k, SLAB)},
            device_id_type=pl.DeviceIdType.MESH,
        )
    for load in loads[2:]:
        load.start()

    size = NH * ATOMS
    same = (iota((size, size), 0) & 15) == (iota((size, size), 1) & 15)
    pair = iota((1, 256), 1)
    i_of = jnp.zeros((1, 256), jnp.int32)
    start = jnp.zeros((1, 256), jnp.int32)
    for i in range(1, NH):
        past = pair >= i * NH - i * (i - 1) // 2
        i_of = i_of + jnp.where(past, 1, 0)
        start = start + jnp.where(past, NH - i + 1, 0)
    j_of = pair - start + i_of
    pick_j = jnp.where((iota((size, 256), 0) >> 4) == j_of, 1.0, 0.0).astype(BF16)
    loads[0].wait()
    loads[1].wait()
    tables[:, :, NPAIR:PAD_P] = jnp.zeros((DEPTH, TILES, PAD_P - NPAIR, 2, 128), BF16)
    for d in range(DEPTH):
        for c in range(TILES):
            pltpu.make_async_copy(
                tab.at[:, d, c], tables.at[d, c, pl.ds(0, NPAIR)], tab_sem.at[d]
            ).start()
    p = pt[...]
    weighted = split(p.astype(F32) * occ[...], 2)
    gram = dot_nt(weighted[0], p) + dot_nt(weighted[1], p)
    spread = jnp.zeros((size, 256), F32)
    for part in split(jnp.where(same, gram, 0.0), 3):
        spread = spread + dot(part, pick_j)
    partial = jnp.zeros((ATOMS, 256), F32)
    for i in range(NH):
        partial = partial + jnp.where(i_of == i, spread[i * ATOMS : (i + 1) * ATOMS], 0.0)
    partial = partial * jnp.where(i_of == j_of, 1.0, 2.0)
    for t in range(4):
        bt[t] = partial[t // 2 * 8 : t // 2 * 8 + 8, t % 2 * 128 : t % 2 * 128 + 128]

    pl.semaphore_wait(barrier, BAND - 1 + 6)

    def send1(t):
        return remote(bt.at[t], rs1.at[me], s1.at[t], r1.at[0], band=4 * t)

    for t in range(4):
        @pl.when(me != 4 * t)
        def _(t=t):
            send1(t).start()

        @pl.when(me == 4 * t)
        def _(t=t):
            rs1[me] = bt[t]

    loads[2].wait()
    pout[:, 0:GXY] = pot[0:16, :].astype(BF16)
    pex[...] = jnp.zeros(pex.shape, F32)
    for r in range(2):
        for c in range(6):
            pex[r * 6 + c : r * 6 + c + 1, :] = pot[16 + r : 17 + r, c * 384 : c * 384 + 384]
    pout[:, GXY : GXY + 384] = pex[...].astype(BF16)
    near = me // 6
    first = DEPTH * me - CZ * near

    def send_pot(half):
        return remote(
            pout, pin.at[half], sp.at[half], rp.at[half],
            slab=lax.rem(slab + SLAB - near - half, SLAB),
        )

    @pl.when(near != 0)
    def _():
        send_pot(0).start()

    @pl.when(near == 0)
    def _():
        pin[0] = pout[...]

    send_pot(1).start()

    tile = me // 4

    def send2(rel):
        return remote(tt.at[tile], tt.at[tile], s2.at[0], r2.at[tile], band=peer(rel))

    def start2(rel, carry):
        send2(rel).start()
        return carry

    @pl.when(lax.rem(me, 4) == 0)
    def _():
        take(r1.at[0], rs1.at[pl.ds(0, BAND - 1)])
        tt[tile] = jnp.sum(rs1[...], axis=0)
        lax.fori_loop(1, BAND, start2, 0)

    for d in range(DEPTH):
        part = tables.at[d, :, pl.ds(0, NPAIR)]
        pltpu.make_async_copy(part, part, tab_sem.at[d]).wait()
    for load in loads[3:]:
        load.wait()

    offset_row = root[...] - slab * CZ
    offset = column(offset_row)
    anchor = column(xy[...])
    species = column(kind[...])
    corner = anchor - GX * ((anchor.astype(F32) + 0.5) * (1.0 / GX)).astype(jnp.int32)
    for d in range(DEPTH):
        anchors[d * ATOMS : (d + 1) * ATOMS, :] = jnp.broadcast_to(anchor, (ATOMS, 128))
        corners[d * ATOMS : (d + 1) * ATOMS, :] = jnp.broadcast_to(corner, (ATOMS, 128))
    mine = jnp.broadcast_to(species, (ATOMS, ROWS)) == (iota((ATOMS, ROWS), 1) & 1)
    to_rows = jnp.where((iota((256, ROWS), 1) >> 1) == iota((256, ROWS), 0), 1.0, 0.0).astype(BF16)

    for t in range(4):
        @pl.when(me != 4 * t)
        def _(t=t):
            remote(tt.at[t], tt.at[t], s2.at[0], r2.at[t], band=4 * t).wait_recv()

    packed = jnp.concatenate(
        [
            jnp.concatenate([tt[0], tt[1]], axis=1),
            jnp.concatenate([tt[2], tt[3]], axis=1),
        ],
        axis=0,
    ).astype(BF16)
    left = jnp.where(mine, dot(packed, to_rows), 0.0).astype(BF16)
    for d in range(DEPTH):
        terms = [dot(left, rows_of(tables, d, c)) for c in range(TILES // 2)]
        for c in range(TILES // 2):
            values[d * ATOMS : (d + 1) * ATOMS, 256 * c : 256 * c + 256] = terms[c]
    rotate(values, anchors, corners, False)
    window = jnp.zeros((WINDOW, GXY), F32)
    for d in range(DEPTH):
        onto = jnp.where(iota((WINDOW, ATOMS), 0) == offset_row + d, 1.0, 0.0).astype(BF16)
        for part in split(values[d * ATOMS : (d + 1) * ATOMS, :], 2):
            window = window + dot(onto, part)
    for j in range(OWNERS):
        ext[j, :, 0:WIDE] = window[0:16, j * WIDE : (j + 1) * WIDE].astype(BF16)
        ends = [window[16:24, j * WIDE + c * 128 : j * WIDE + c * 128 + 128] for c in range(3)]
        ends = jnp.concatenate([ends[0] + pltpu.roll(ends[1], 4, 0), ends[2]], axis=0)
        ext[j, :, WIDE : WIDE + 128] = ends.astype(BF16)

    def send3(j):
        return remote(ext.at[j], rs3.at[me], s3.at[j], r3.at[0], band=8 * j // 3)

    for j in range(OWNERS):
        @pl.when(me != 8 * j // 3)
        def _(j=j):
            send3(j).start()

        @pl.when(me == 8 * j // 3)
        def _(j=j):
            rs3[me] = ext[j]

    @pl.when(near != 0)
    def _():
        send_pot(0).wait_recv()

    send_pot(1).wait_recv()
    extra = []
    for half in range(2):
        packed_rows = pin[half, :, GXY : GXY + 384].astype(F32)
        for r in range(2):
            extra.append(
                jnp.concatenate([packed_rows[r * 6 + c : r * 6 + c + 1] for c in range(6)], axis=1)
            )
    extra = jnp.concatenate(extra + [jnp.zeros((12, GXY), F32)], axis=0).astype(BF16)
    planes = jnp.concatenate([pin[0, :, 0:GXY], pin[1, :, 0:GXY], extra], axis=0)
    for d in range(DEPTH):
        target = offset + (first + d)
        late = jnp.where(target >= CZ, 1, 0)
        row = target - CZ * late
        source = jnp.where(row < 16, 16 * late + row, 32 + 2 * late + row - 16)
        choose = jnp.where(
            iota((ATOMS, 48), 1) == jnp.broadcast_to(source, (ATOMS, 48)), 1.0, 0.0
        ).astype(BF16)
        values[d * ATOMS : (d + 1) * ATOMS, :] = dot(choose, planes)
    rotate(values, anchors, corners, True)
    for d in range(DEPTH):
        boxes[d] = values[d * ATOMS : (d + 1) * ATOMS, :].astype(BF16)

    mark = (3 * me + 7) // 8
    owner = jnp.logical_and(mark < OWNERS, 8 * mark // 3 == me)
    own = jnp.minimum(mark, OWNERS - 1)

    def send4(k):
        return remote(
            st.at[k], p4.at[k - 1], s4.at[k - 1], r4.at[k - 1], slab=lax.rem(slab + k, SLAB)
        )

    def send5(rel):
        return remote(ag.at[own], ag.at[own], s5.at[0], r5.at[own], band=peer(rel))

    def start5(rel, carry):
        send5(rel).start()
        return carry

    @pl.when(owner)
    def _():
        out_row = iota((4 * WINDOW, 256), 0)
        block = jnp.zeros(out_row.shape, jnp.int32)
        for k in (1, 2, 3):
            block = block + jnp.where(out_row >= k * WINDOW, 1, 0)
        out_row = out_row - WINDOW * block
        plane = jnp.where(out_row < CZ, out_row + CZ * block, -1)
        source = iota((4 * WINDOW, 256), 1)
        base = DEPTH * (source >> 4)
        source = source & 15
        gather = jnp.where(plane == base + source, 1.0, 0.0).astype(BF16)
        tails = [
            jnp.where(
                jnp.logical_and(source >> 2 == c, plane == base + 16 + (source & 3)), 1.0, 0.0
            ).astype(BF16)
            for c in range(3)
        ]
        take(r3.at[0], rs3.at[pl.ds(0, BAND - 1)])
        end = rs3[:, :, WIDE : WIDE + 128].reshape(256, 128)
        whole = dot(gather, rs3[:, :, 0:WIDE].reshape(256, WIDE))
        whole = whole + jnp.concatenate([dot(tails[c], end) for c in range(3)], axis=1)
        for k in range(4):
            st[k] = whole[k * WINDOW : (k + 1) * WINDOW]
        for k in (1, 2, 3):
            send4(k).start()

    sums = jnp.zeros((ATOMS, ROWS), F32)
    for d in range(DEPTH):
        for c in range(TILES // 2):
            sums = sums + dot_nt(boxes[d, :, 256 * c : 256 * c + 256], rows_of(tables, d, c))
    folded = jnp.zeros((ATOMS, 256), F32)
    for part in split(jnp.where(mine, sums, 0.0), 3):
        folded = folded + dot_nt(part, to_rows)
    for a in range(ATOMS):
        isnd[a] = folded[a : a + 1]

    def send6(rel):
        other = peer(rel)
        return remote(isnd.at[other], ircv.at[me], s6.at[0], r6.at[0], band=other)

    def start6(rel, carry):
        send6(rel).start()
        return carry

    @pl.when(owner)
    def _():
        for k in (1, 2, 3):
            send4(k).wait_recv()
        total = st[0] + p4[0] + p4[1] + p4[2]
        ends = [total[16:24, c * 128 : c * 128 + 128] for c in range(3)]
        ends = ends[0] + pltpu.roll(ends[1], 2, 0) + pltpu.roll(ends[2], 4, 0)
        ends = jnp.concatenate([ends, jnp.zeros_like(ends)], axis=0)
        ag[own, :, 0:WIDE] = total[0:16].astype(BF16)
        ag[own, :, WIDE : WIDE + 128] = ends.astype(BF16)
        lax.fori_loop(1, BAND, start5, 0)

    lax.fori_loop(1, BAND, start6, 0)
    ircv[me] = isnd[me]

    take(r6.at[0], ircv.at[pl.ds(0, BAND - 1)])
    ints[...] = jnp.sum(ircv[...], axis=0)

    for j in range(OWNERS):
        @pl.when(me != 8 * j // 3)
        def _(j=j):
            remote(ag.at[j], ag.at[j], s5.at[0], r5.at[j], band=8 * j // 3).wait_recv()

        dens[0:16, j * WIDE : (j + 1) * WIDE] = ag[j, :, 0:WIDE]
        ends = ag[j, :, WIDE : WIDE + 128].astype(F32)[0:8]
        for c in range(3):
            at = j * WIDE + c * 128
            tail = pltpu.roll(ends, 8 - 2 * c, 0) if c else ends
            tail = jnp.concatenate([tail, jnp.zeros_like(tail)], axis=0)
            dens[16:32, at : at + 128] = tail.astype(BF16)

    for t in range(4):
        @pl.when(me != 4 * t)
        def _(t=t):
            send1(t).wait_send()

    @pl.when(near != 0)
    def _():
        send_pot(0).wait_send()

    send_pot(1).wait_send()

    @pl.when(lax.rem(me, 4) == 0)
    def _():
        take(s2.at[0], rs1.at[pl.ds(0, BAND - 1)])

    for j in range(OWNERS):
        @pl.when(me != 8 * j // 3)
        def _(j=j):
            send3(j).wait_send()

    take(s6.at[0], ircv.at[pl.ds(0, BAND - 1)])

    @pl.when(owner)
    def _():
        for k in (1, 2, 3):
            send4(k).wait_send()
        take(s5.at[0], rs3.at[pl.ds(0, BAND - 1)])


def shards(projections, occupation, augment_tables, box_root, box_xy, species, potential):
    pt = jnp.transpose(projections, (1, 2, 0)).reshape(NH * ATOMS, 256)
    tab = jnp.transpose(augment_tables.reshape(2, NPAIR, DEPTH, TILES, 128), (1, 2, 3, 0, 4))
    vmem = pl.BlockSpec(memory_space=pltpu.VMEM)
    dma = pltpu.SemaphoreType.DMA
    density, integrals = pl.pallas_call(
        kernel,
        out_shape=(
            jax.ShapeDtypeStruct((32, GXY), BF16),
            jax.ShapeDtypeStruct((1, 256), F32),
        ),
        in_specs=[pl.BlockSpec(memory_space=pltpu.HBM)] * 7,
        out_specs=(vmem, vmem),
        scratch_shapes=[
            pltpu.VMEM((NH * ATOMS, 256), BF16),
            pltpu.VMEM((1, 256), F32),
            pltpu.VMEM((1, ATOMS), jnp.int32),
            pltpu.VMEM((1, ATOMS), jnp.int32),
            pltpu.VMEM((1, ATOMS), jnp.int32),
            pltpu.VMEM((CZ, GXY), F32),
            pltpu.VMEM((DEPTH, TILES, PAD_P, 2, 128), BF16),
            pltpu.VMEM((4, 8, 128), F32),
            pltpu.VMEM((BAND, 8, 128), F32),
            pltpu.VMEM((4, 8, 128), F32),
            pltpu.VMEM((16, 384), F32),
            pltpu.VMEM((16, GXY + 384), BF16),
            pltpu.VMEM((2, 16, GXY + 384), BF16),
            pltpu.VMEM((DEPTH, ATOMS, GXY), BF16),
            pltpu.VMEM((OWNERS, 16, WIDE + 128), BF16),
            pltpu.VMEM((BAND, 16, WIDE + 128), BF16),
            pltpu.VMEM((4, WINDOW, WIDE), F32),
            pltpu.VMEM((3, WINDOW, WIDE), F32),
            pltpu.VMEM((DEPTH * ATOMS, GXY), F32),
            pltpu.VMEM((DEPTH * ATOMS, 128), jnp.int32),
            pltpu.VMEM((DEPTH * ATOMS, 128), jnp.int32),
            pltpu.VMEM((OWNERS, 16, WIDE + 128), BF16),
            pltpu.VMEM((ATOMS, 1, 256), F32),
            pltpu.VMEM((BAND, 1, 256), F32),
            dma((6,)),
            dma((DEPTH,)),
            dma((4,)), dma((1,)),
            dma((1,)), dma((4,)),
            dma((2,)), dma((2,)),
            dma((OWNERS,)), dma((1,)),
            dma((3,)), dma((3,)),
            dma((1,)), dma((OWNERS,)),
            dma((1,)), dma((1,)),
        ],
        compiler_params=pltpu.CompilerParams(
            collective_id=0, has_side_effects=True, vmem_limit_bytes=56 << 20
        ),
    )(
        pt,
        occupation.reshape(1, 256),
        box_root.reshape(1, ATOMS),
        box_xy.reshape(1, ATOMS),
        species.reshape(1, ATOMS),
        potential,
        tab,
    )
    return density[0:CZ].astype(F32), integrals[:, 0:NPAIR].reshape(NPAIR, 1)


def solution(mesh):
    placed = (
        P("band", None, "slab"),
        P("band"),
        P(None, None, "band", None),
        P("slab"),
        P("slab"),
        P("slab"),
        P("slab", None),
    )
    return jax.shard_map(
        shards,
        mesh=mesh,
        in_specs=placed,
        out_specs=(P("slab", None), P(None, ("slab", "band"))),
        check_vma=False,
    )
```

```python
import jax
import jax.numpy as jnp
from jax import lax
from jax.experimental import pallas as pl
from jax.experimental.pallas import tpu as pltpu
from jax.sharding import PartitionSpec as P

GX = 48
GXY = 2304
NH = 18
NPAIR = 171
DEPTH = 3
CZ = 18
ATOMS = 16
BAND = 16
SLAB = 32
PAD_P = 176
ROWS = 2 * PAD_P
OWNERS = 6
WIDE = GXY // OWNERS
WINDOW = 24
TILES = 18
SPREAD = 6
EARLY = 8
F32 = jnp.float32
BF16 = jnp.bfloat16
NT = (((1,), (1,)), ((), ()))


def iota(shape, axis):
    return lax.broadcasted_iota(jnp.int32, shape, axis)


def dot(a, b):
    return jnp.dot(a, b, preferred_element_type=F32)


def dot_nt(a, b):
    return lax.dot_general(a, b, NT, preferred_element_type=F32)


def split(x, terms):
    parts = []
    for _ in range(terms):
        part = x.astype(BF16)
        parts.append(part)
        x = x - part.astype(F32)
    return parts


def column(row):
    picked = jnp.where(iota((ATOMS, ATOMS), 0) == iota((ATOMS, ATOMS), 1), row.astype(F32), 0.0)
    return jnp.sum(picked, axis=1, keepdims=True).astype(jnp.int32)


def rows_of(tables, d, c):
    return jnp.concatenate(
        [tables[d, 2 * c].reshape(ROWS, 128), tables[d, 2 * c + 1].reshape(ROWS, 128)], axis=1
    )


def take(sem, landed):
    pltpu.make_async_copy(landed, landed, sem).wait()


def rotate(values, anchors, corners, left):
    lane = iota((8, 128), 1)

    def turn(v, step):
        back = GXY - step if left else step
        back = back % 128
        turned = [pltpu.roll(x, back, 1) for x in v]
        if left:
            return [jnp.where(lane < back, turned[c], turned[(c + 1) % TILES]) for c in range(TILES)]
        return [jnp.where(lane >= back, turned[c], turned[c - 1]) for c in range(TILES)]

    def eight_rows(i, carry):
        rows = pl.ds(pl.multiple_of(8 * i, 8), 8)
        amount = anchors[rows, :]
        v = [values[rows, 128 * c : 128 * c + 128] for c in range(TILES)]
        for bit in range(12):
            on = (amount & (1 << bit)) != 0
            if bit < 7:
                moved = turn(v, 1 << bit)
            else:
                hop = 1 << (bit - 7)
                moved = [v[(c + hop if left else c - hop) % TILES] for c in range(TILES)]
            v = [jnp.where(on, moved[c], v[c]) for c in range(TILES)]
        corner = corners[rows, :]
        inside = []
        for c in range(3):
            line = lane + 128 * c % GX
            for end in (GX, 2 * GX, 3 * GX):
                line = line - jnp.where(lane + 128 * c % GX >= end, GX, 0)
            inside.append(line < GX - corner if left else line >= corner)
        wrap = [pltpu.roll(x, GX if left else 128 - GX, 1) for x in v]
        for c in range(TILES):
            if left:
                wrapped = jnp.where(lane >= GX, wrap[c], wrap[c - 1])
            else:
                wrapped = jnp.where(lane < 128 - GX, wrap[c], wrap[(c + 1) % TILES])
            values[rows, 128 * c : 128 * c + 128] = jnp.where(inside[c % 3], v[c], wrapped)
        return carry

    lax.fori_loop(0, DEPTH * ATOMS // 8, eight_rows, 0)


def remote(src, dst, send, recv, **where):
    return pltpu.make_async_remote_copy(
        src_ref=src,
        dst_ref=dst,
        send_sem=send,
        recv_sem=recv,
        device_id=where,
        device_id_type=pl.DeviceIdType.MESH,
    )


def kernel(
    pt_hbm, occ_hbm, root_hbm, xy_hbm, kind_hbm, pot_hbm, tab, dens, ints,
    pt, occ, root, xy, kind, pot, raw, tables, bt, rs1, tt, pex, pout, pin, boxes, ext, rs3, st, p4, values, anchors, corners, ag, isnd, ircv,
    in_sem, raw_sem, tab_sem, s1, r1, s2, r2, sp, rp, s3, r3, s4, r4, s5, r5, s6, r6,
):
    me = lax.axis_index("band")
    slab = lax.axis_index("slab")

    def peer(rel):
        return lax.rem(me + rel, BAND)

    loads = [
        pltpu.make_async_copy(src, dst, in_sem.at[n])
        for n, (src, dst) in enumerate(
            [(pt_hbm, pt), (occ_hbm, occ), (pot_hbm, pot), (root_hbm, root), (xy_hbm, xy), (kind_hbm, kind)]
        )
    ]
    loads[0].start()
    loads[1].start()
    barrier = pltpu.get_barrier_semaphore()

    def greet(rel, carry):
        pl.semaphore_signal(
            barrier, inc=1, device_id={"band": peer(rel)}, device_id_type=pl.DeviceIdType.MESH
        )
        return carry

    lax.fori_loop(1, BAND, greet, 0)
    for k in (1, 2, 3, SLAB - 3, SLAB - 2, SLAB - 1):
        pl.semaphore_signal(
            barrier, inc=1, device_id={"slab": lax.rem(slab + k, SLAB)},
            device_id_type=pl.DeviceIdType.MESH,
        )
    for load in loads[2:]:
        load.start()
    whole = pltpu.make_async_copy(tab.at[:, :, pl.ds(SPREAD, TILES - SPREAD)], raw.at[pl.ds(0, NPAIR)], raw_sem)
    whole.start()
    for d in range(DEPTH):
        for c in range(SPREAD):
            pltpu.make_async_copy(
                tab.at[:, d, c], tables.at[d, c, pl.ds(0, NPAIR)], tab_sem.at[d]
            ).start()
    tables[:, 0:SPREAD, NPAIR:PAD_P] = jnp.zeros((DEPTH, SPREAD, PAD_P - NPAIR, 2, 128), BF16)
    raw[NPAIR:PAD_P] = jnp.zeros((PAD_P - NPAIR, DEPTH, TILES - SPREAD, 2, 128), BF16)

    size = NH * ATOMS
    same = (iota((size, size), 0) & 15) == (iota((size, size), 1) & 15)
    pair = iota((1, 256), 1)
    i_of = jnp.zeros((1, 256), jnp.int32)
    start = jnp.zeros((1, 256), jnp.int32)
    for i in range(1, NH):
        past = pair >= i * NH - i * (i - 1) // 2
        i_of = i_of + jnp.where(past, 1, 0)
        start = start + jnp.where(past, NH - i + 1, 0)
    j_of = pair - start + i_of
    pick_j = jnp.where((iota((size, 256), 0) >> 4) == j_of, 1.0, 0.0).astype(BF16)
    loads[0].wait()
    loads[1].wait()
    p = pt[...]
    weighted = split(p.astype(F32) * occ[...], 2)
    gram = dot_nt(weighted[0], p) + dot_nt(weighted[1], p)
    spread = jnp.zeros((size, 256), F32)
    for part in split(jnp.where(same, gram, 0.0), 3):
        spread = spread + dot(part, pick_j)
    partial = jnp.zeros((ATOMS, 256), F32)
    for i in range(NH):
        partial = partial + jnp.where(i_of == i, spread[i * ATOMS : (i + 1) * ATOMS], 0.0)
    partial = partial * jnp.where(i_of == j_of, 1.0, 2.0)
    for t in range(4):
        bt[t] = partial[t // 2 * 8 : t // 2 * 8 + 8, t % 2 * 128 : t % 2 * 128 + 128]

    pl.semaphore_wait(barrier, BAND - 1 + 6)

    def send1(t):
        return remote(bt.at[t], rs1.at[me], s1.at[t], r1.at[0], band=4 * t)

    for t in range(4):
        @pl.when(me != 4 * t)
        def _(t=t):
            send1(t).start()

        @pl.when(me == 4 * t)
        def _(t=t):
            rs1[me] = bt[t]

    loads[2].wait()
    pout[:, 0:GXY] = pot[0:16, :].astype(BF16)
    pex[...] = jnp.zeros(pex.shape, F32)
    for r in range(2):
        for c in range(6):
            pex[r * 6 + c : r * 6 + c + 1, :] = pot[16 + r : 17 + r, c * 384 : c * 384 + 384]
    pout[:, GXY : GXY + 384] = pex[...].astype(BF16)
    near = me // 6
    first = DEPTH * me - CZ * near

    def send_pot(half):
        return remote(
            pout, pin.at[half], sp.at[half], rp.at[half],
            slab=lax.rem(slab + SLAB - near - half, SLAB),
        )

    @pl.when(near != 0)
    def _():
        send_pot(0).start()

    @pl.when(near == 0)
    def _():
        pin[0] = pout[...]

    send_pot(1).start()

    def regroup(n, carry):
        for d in range(DEPTH):
            for c in range(TILES - SPREAD):
                tables[d, SPREAD + c, pl.ds(8 * n, 8)] = raw[pl.ds(8 * n, 8), d, c]
        return carry

    whole.wait()
    lax.fori_loop(0, EARLY, regroup, 0)

    tile = me // 4

    def send2(rel):
        return remote(tt.at[tile], tt.at[tile], s2.at[0], r2.at[tile], band=peer(rel))

    def start2(rel, carry):
        send2(rel).start()
        return carry

    @pl.when(lax.rem(me, 4) == 0)
    def _():
        take(r1.at[0], rs1.at[pl.ds(0, BAND - 1)])
        tt[tile] = jnp.sum(rs1[...], axis=0)
        lax.fori_loop(1, BAND, start2, 0)

    lax.fori_loop(EARLY, PAD_P // 8, regroup, 0)
    for d in range(DEPTH):
        part = tables.at[d, pl.ds(0, SPREAD), pl.ds(0, NPAIR)]
        pltpu.make_async_copy(part, part, tab_sem.at[d]).wait()
    for load in loads[3:]:
        load.wait()

    offset_row = root[...] - slab * CZ
    offset = column(offset_row)
    anchor = column(xy[...])
    species = column(kind[...])
    corner = anchor - GX * ((anchor.astype(F32) + 0.5) * (1.0 / GX)).astype(jnp.int32)
    for d in range(DEPTH):
        anchors[d * ATOMS : (d + 1) * ATOMS, :] = jnp.broadcast_to(anchor, (ATOMS, 128))
        corners[d * ATOMS : (d + 1) * ATOMS, :] = jnp.broadcast_to(corner, (ATOMS, 128))
    mine = jnp.broadcast_to(species, (ATOMS, ROWS)) == (iota((ATOMS, ROWS), 1) & 1)
    to_rows = jnp.where((iota((256, ROWS), 1) >> 1) == iota((256, ROWS), 0), 1.0, 0.0).astype(BF16)

    for t in range(4):
        @pl.when(me != 4 * t)
        def _(t=t):
            remote(tt.at[t], tt.at[t], s2.at[0], r2.at[t], band=4 * t).wait_recv()

    packed = jnp.concatenate(
        [
            jnp.concatenate([tt[0], tt[1]], axis=1),
            jnp.concatenate([tt[2], tt[3]], axis=1),
        ],
        axis=0,
    ).astype(BF16)
    left = jnp.where(mine, dot(packed, to_rows), 0.0).astype(BF16)
    for d in range(DEPTH):
        terms = [dot(left, rows_of(tables, d, c)) for c in range(TILES // 2)]
        for c in range(TILES // 2):
            values[d * ATOMS : (d + 1) * ATOMS, 256 * c : 256 * c + 256] = terms[c]
    rotate(values, anchors, corners, False)
    window = jnp.zeros((WINDOW, GXY), F32)
    for d in range(DEPTH):
        onto = jnp.where(iota((WINDOW, ATOMS), 0) == offset_row + d, 1.0, 0.0).astype(BF16)
        for part in split(values[d * ATOMS : (d + 1) * ATOMS, :], 2):
            window = window + dot(onto, part)
    for j in range(OWNERS):
        ext[j, :, 0:WIDE] = window[0:16, j * WIDE : (j + 1) * WIDE].astype(BF16)
        ends = [window[16:24, j * WIDE + c * 128 : j * WIDE + c * 128 + 128] for c in range(3)]
        ends = jnp.concatenate([ends[0] + pltpu.roll(ends[1], 4, 0), ends[2]], axis=0)
        ext[j, :, WIDE : WIDE + 128] = ends.astype(BF16)

    def send3(j):
        return remote(ext.at[j], rs3.at[me], s3.at[j], r3.at[0], band=8 * j // 3)

    for j in range(OWNERS):
        @pl.when(me != 8 * j // 3)
        def _(j=j):
            send3(j).start()

        @pl.when(me == 8 * j // 3)
        def _(j=j):
            rs3[me] = ext[j]

    @pl.when(near != 0)
    def _():
        send_pot(0).wait_recv()

    send_pot(1).wait_recv()
    extra = []
    for half in range(2):
        packed_rows = pin[half, :, GXY : GXY + 384].astype(F32)
        for r in range(2):
            extra.append(
                jnp.concatenate([packed_rows[r * 6 + c : r * 6 + c + 1] for c in range(6)], axis=1)
            )
    extra = jnp.concatenate(extra + [jnp.zeros((12, GXY), F32)], axis=0).astype(BF16)
    planes = jnp.concatenate([pin[0, :, 0:GXY], pin[1, :, 0:GXY], extra], axis=0)
    for d in range(DEPTH):
        target = offset + (first + d)
        late = jnp.where(target >= CZ, 1, 0)
        row = target - CZ * late
        source = jnp.where(row < 16, 16 * late + row, 32 + 2 * late + row - 16)
        choose = jnp.where(
            iota((ATOMS, 48), 1) == jnp.broadcast_to(source, (ATOMS, 48)), 1.0, 0.0
        ).astype(BF16)
        values[d * ATOMS : (d + 1) * ATOMS, :] = dot(choose, planes)
    rotate(values, anchors, corners, True)
    for d in range(DEPTH):
        boxes[d] = values[d * ATOMS : (d + 1) * ATOMS, :].astype(BF16)

    mark = (3 * me + 7) // 8
    owner = jnp.logical_and(mark < OWNERS, 8 * mark // 3 == me)
    own = jnp.minimum(mark, OWNERS - 1)

    def send4(k):
        return remote(
            st.at[k], p4.at[k - 1], s4.at[k - 1], r4.at[k - 1], slab=lax.rem(slab + k, SLAB)
        )

    def send5(rel):
        return remote(ag.at[own], ag.at[own], s5.at[0], r5.at[own], band=peer(rel))

    def start5(rel, carry):
        send5(rel).start()
        return carry

    @pl.when(owner)
    def _():
        out_row = iota((4 * WINDOW, 256), 0)
        block = jnp.zeros(out_row.shape, jnp.int32)
        for k in (1, 2, 3):
            block = block + jnp.where(out_row >= k * WINDOW, 1, 0)
        out_row = out_row - WINDOW * block
        plane = jnp.where(out_row < CZ, out_row + CZ * block, -1)
        source = iota((4 * WINDOW, 256), 1)
        base = DEPTH * (source >> 4)
        source = source & 15
        gather = jnp.where(plane == base + source, 1.0, 0.0).astype(BF16)
        tails = [
            jnp.where(
                jnp.logical_and(source >> 2 == c, plane == base + 16 + (source & 3)), 1.0, 0.0
            ).astype(BF16)
            for c in range(3)
        ]
        take(r3.at[0], rs3.at[pl.ds(0, BAND - 1)])
        end = rs3[:, :, WIDE : WIDE + 128].reshape(256, 128)
        summed = dot(gather, rs3[:, :, 0:WIDE].reshape(256, WIDE))
        summed = summed + jnp.concatenate([dot(tails[c], end) for c in range(3)], axis=1)
        for k in range(4):
            st[k] = summed[k * WINDOW : (k + 1) * WINDOW]
        for k in (1, 2, 3):
            send4(k).start()

    sums = jnp.zeros((ATOMS, ROWS), F32)
    for d in range(DEPTH):
        for c in range(TILES // 2):
            sums = sums + dot_nt(boxes[d, :, 256 * c : 256 * c + 256], rows_of(tables, d, c))
    folded = jnp.zeros((ATOMS, 256), F32)
    for part in split(jnp.where(mine, sums, 0.0), 3):
        folded = folded + dot_nt(part, to_rows)
    for a in range(ATOMS):
        isnd[a] = folded[a : a + 1]

    def send6(rel):
        other = peer(rel)
        return remote(isnd.at[other], ircv.at[me], s6.at[0], r6.at[0], band=other)

    def start6(rel, carry):
        send6(rel).start()
        return carry

    @pl.when(owner)
    def _():
        for k in (1, 2, 3):
            send4(k).wait_recv()
        total = st[0] + p4[0] + p4[1] + p4[2]
        ends = [total[16:24, c * 128 : c * 128 + 128] for c in range(3)]
        ends = ends[0] + pltpu.roll(ends[1], 2, 0) + pltpu.roll(ends[2], 4, 0)
        ends = jnp.concatenate([ends, jnp.zeros_like(ends)], axis=0)
        ag[own, :, 0:WIDE] = total[0:16].astype(BF16)
        ag[own, :, WIDE : WIDE + 128] = ends.astype(BF16)
        lax.fori_loop(1, BAND, start5, 0)

    lax.fori_loop(1, BAND, start6, 0)
    ircv[me] = isnd[me]

    take(r6.at[0], ircv.at[pl.ds(0, BAND - 1)])
    ints[...] = jnp.sum(ircv[...], axis=0)

    for j in range(OWNERS):
        @pl.when(me != 8 * j // 3)
        def _(j=j):
            remote(ag.at[j], ag.at[j], s5.at[0], r5.at[j], band=8 * j // 3).wait_recv()

        dens[0:16, j * WIDE : (j + 1) * WIDE] = ag[j, :, 0:WIDE]
        ends = ag[j, :, WIDE : WIDE + 128].astype(F32)[0:8]
        for c in range(3):
            at = j * WIDE + c * 128
            tail = pltpu.roll(ends, 8 - 2 * c, 0) if c else ends
            tail = jnp.concatenate([tail, jnp.zeros_like(tail)], axis=0)
            dens[16:32, at : at + 128] = tail.astype(BF16)

    for t in range(4):
        @pl.when(me != 4 * t)
        def _(t=t):
            send1(t).wait_send()

    @pl.when(near != 0)
    def _():
        send_pot(0).wait_send()

    send_pot(1).wait_send()

    @pl.when(lax.rem(me, 4) == 0)
    def _():
        take(s2.at[0], rs1.at[pl.ds(0, BAND - 1)])

    for j in range(OWNERS):
        @pl.when(me != 8 * j // 3)
        def _(j=j):
            send3(j).wait_send()

    take(s6.at[0], ircv.at[pl.ds(0, BAND - 1)])

    @pl.when(owner)
    def _():
        for k in (1, 2, 3):
            send4(k).wait_send()
        take(s5.at[0], rs3.at[pl.ds(0, BAND - 1)])


def shards(projections, occupation, augment_tables, box_root, box_xy, species, potential):
    pt = jnp.transpose(projections, (1, 2, 0)).reshape(NH * ATOMS, 256)
    tab = jnp.transpose(augment_tables.reshape(2, NPAIR, DEPTH, TILES, 128), (1, 2, 3, 0, 4))
    vmem = pl.BlockSpec(memory_space=pltpu.VMEM)
    dma = pltpu.SemaphoreType.DMA
    density, integrals = pl.pallas_call(
        kernel,
        out_shape=(
            jax.ShapeDtypeStruct((32, GXY), BF16),
            jax.ShapeDtypeStruct((1, 256), F32),
        ),
        in_specs=[pl.BlockSpec(memory_space=pltpu.HBM)] * 7,
        out_specs=(vmem, vmem),
        scratch_shapes=[
            pltpu.VMEM((NH * ATOMS, 256), BF16),
            pltpu.VMEM((1, 256), F32),
            pltpu.VMEM((1, ATOMS), jnp.int32),
            pltpu.VMEM((1, ATOMS), jnp.int32),
            pltpu.VMEM((1, ATOMS), jnp.int32),
            pltpu.VMEM((CZ, GXY), F32),
            pltpu.VMEM((PAD_P, DEPTH, TILES - SPREAD, 2, 128), BF16),
            pltpu.VMEM((DEPTH, TILES, PAD_P, 2, 128), BF16),
            pltpu.VMEM((4, 8, 128), F32),
            pltpu.VMEM((BAND, 8, 128), F32),
            pltpu.VMEM((4, 8, 128), F32),
            pltpu.VMEM((16, 384), F32),
            pltpu.VMEM((16, GXY + 384), BF16),
            pltpu.VMEM((2, 16, GXY + 384), BF16),
            pltpu.VMEM((DEPTH, ATOMS, GXY), BF16),
            pltpu.VMEM((OWNERS, 16, WIDE + 128), BF16),
            pltpu.VMEM((BAND, 16, WIDE + 128), BF16),
            pltpu.VMEM((4, WINDOW, WIDE), F32),
            pltpu.VMEM((3, WINDOW, WIDE), F32),
            pltpu.VMEM((DEPTH * ATOMS, GXY), F32),
            pltpu.VMEM((DEPTH * ATOMS, 128), jnp.int32),
            pltpu.VMEM((DEPTH * ATOMS, 128), jnp.int32),
            pltpu.VMEM((OWNERS, 16, WIDE + 128), BF16),
            pltpu.VMEM((ATOMS, 1, 256), F32),
            pltpu.VMEM((BAND, 1, 256), F32),
            dma((6,)),
            dma,
            dma((DEPTH,)),
            dma((4,)), dma((1,)),
            dma((1,)), dma((4,)),
            dma((2,)), dma((2,)),
            dma((OWNERS,)), dma((1,)),
            dma((3,)), dma((3,)),
            dma((1,)), dma((OWNERS,)),
            dma((1,)), dma((1,)),
        ],
        compiler_params=pltpu.CompilerParams(
            collective_id=0, has_side_effects=True, vmem_limit_bytes=56 << 20
        ),
    )(
        pt,
        occupation.reshape(1, 256),
        box_root.reshape(1, ATOMS),
        box_xy.reshape(1, ATOMS),
        species.reshape(1, ATOMS),
        potential,
        tab,
    )
    return density[0:CZ].astype(F32), integrals[:, 0:NPAIR].reshape(NPAIR, 1)


def solution(mesh):
    placed = (
        P("band", None, "slab"),
        P("band"),
        P(None, None, "band", None),
        P("slab"),
        P("slab"),
        P("slab"),
        P("slab", None),
    )
    return jax.shard_map(
        shards,
        mesh=mesh,
        in_specs=placed,
        out_specs=(P("slab", None), P(None, ("slab", "band"))),
        check_vma=False,
    )
```

```python
import jax
import jax.numpy as jnp
from jax import lax
from jax.experimental import pallas as pl
from jax.experimental.pallas import tpu as pltpu
from jax.sharding import PartitionSpec as P

GX = 48
GXY = 2304
NH = 18
NPAIR = 171
DEPTH = 3
CZ = 18
ATOMS = 16
BAND = 16
SLAB = 32
PAD_P = 176
ROWS = 2 * PAD_P
OWNERS = 6
WIDE = GXY // OWNERS
WINDOW = 24
TILES = 18
F32 = jnp.float32
BF16 = jnp.bfloat16
NT = (((1,), (1,)), ((), ()))


def iota(shape, axis):
    return lax.broadcasted_iota(jnp.int32, shape, axis)


def dot(a, b):
    return jnp.dot(a, b, preferred_element_type=F32)


def dot_nt(a, b):
    return lax.dot_general(a, b, NT, preferred_element_type=F32)


def split(x, terms):
    parts = []
    for _ in range(terms):
        part = x.astype(BF16)
        parts.append(part)
        x = x - part.astype(F32)
    return parts


def column(row):
    picked = jnp.where(iota((ATOMS, ATOMS), 0) == iota((ATOMS, ATOMS), 1), row.astype(F32), 0.0)
    return jnp.sum(picked, axis=1, keepdims=True).astype(jnp.int32)


def rows_of(tables, d, c):
    return jnp.concatenate(
        [tables[d, 2 * c].reshape(ROWS, 128), tables[d, 2 * c + 1].reshape(ROWS, 128)], axis=1
    )


def take(sem, landed):
    pltpu.make_async_copy(landed, landed, sem).wait()


def rotate(values, amount, left):
    amount = jnp.broadcast_to(amount, values.shape)
    for bit in range(12):
        step = 1 << bit
        turned = pltpu.roll(values, GXY - step if left else step, 1)
        values = jnp.where((amount & step) != 0, turned, values)
    return values


def remote(src, dst, send, recv, **where):
    return pltpu.make_async_remote_copy(
        src_ref=src,
        dst_ref=dst,
        send_sem=send,
        recv_sem=recv,
        device_id=where,
        device_id_type=pl.DeviceIdType.MESH,
    )


def kernel(
    pt_hbm, occ_hbm, root_hbm, xy_hbm, kind_hbm, pot_hbm, tab, dens, ints,
    pt, occ, root, xy, kind, pot, tables, bt, rs1, tt, pex, pout, pin, boxes, ext, rs3, st, p4, ag, isnd, ircv,
    in_sem, tab_sem, s1, r1, s2, r2, sp, rp, s3, r3, s4, r4, s5, r5, s6, r6,
):
    me = lax.axis_index("band")
    slab = lax.axis_index("slab")

    def peer(rel):
        return lax.rem(me + rel, BAND)

    loads = [
        pltpu.make_async_copy(src, dst, in_sem.at[n])
        for n, (src, dst) in enumerate(
            [(pt_hbm, pt), (occ_hbm, occ), (pot_hbm, pot), (root_hbm, root), (xy_hbm, xy), (kind_hbm, kind)]
        )
    ]
    loads[0].start()
    loads[1].start()
    barrier = pltpu.get_barrier_semaphore()

    def greet(rel, carry):
        pl.semaphore_signal(
            barrier, inc=1, device_id={"band": peer(rel)}, device_id_type=pl.DeviceIdType.MESH
        )
        return carry

    lax.fori_loop(1, BAND, greet, 0)
    for k in (1, 2, 3, SLAB - 3, SLAB - 2, SLAB - 1):
        pl.semaphore_signal(
            barrier, inc=1, device_id={"slab": lax.rem(slab + k, SLAB)},
            device_id_type=pl.DeviceIdType.MESH,
        )
    for load in loads[2:]:
        load.start()
    tables[:, :, NPAIR:PAD_P] = jnp.zeros((DEPTH, TILES, PAD_P - NPAIR, 2, 128), BF16)
    for d in range(DEPTH):
        for c in range(TILES):
            pltpu.make_async_copy(
                tab.at[:, d, c], tables.at[d, c, pl.ds(0, NPAIR)], tab_sem.at[d]
            ).start()

    size = NH * ATOMS
    same = (iota((size, size), 0) & 15) == (iota((size, size), 1) & 15)
    pair = iota((1, 256), 1)
    i_of = jnp.zeros((1, 256), jnp.int32)
    start = jnp.zeros((1, 256), jnp.int32)
    for i in range(1, NH):
        past = pair >= i * NH - i * (i - 1) // 2
        i_of = i_of + jnp.where(past, 1, 0)
        start = start + jnp.where(past, NH - i + 1, 0)
    j_of = pair - start + i_of
    pick_j = jnp.where((iota((size, 256), 0) >> 4) == j_of, 1.0, 0.0).astype(BF16)
    loads[0].wait()
    loads[1].wait()
    p = pt[...]
    weighted = split(p.astype(F32) * occ[...], 2)
    gram = dot_nt(weighted[0], p) + dot_nt(weighted[1], p)
    spread = jnp.zeros((size, 256), F32)
    for part in split(jnp.where(same, gram, 0.0), 3):
        spread = spread + dot(part, pick_j)
    partial = jnp.zeros((ATOMS, 256), F32)
    for i in range(NH):
        partial = partial + jnp.where(i_of == i, spread[i * ATOMS : (i + 1) * ATOMS], 0.0)
    partial = partial * jnp.where(i_of == j_of, 1.0, 2.0)
    for t in range(4):
        bt[t] = partial[t // 2 * 8 : t // 2 * 8 + 8, t % 2 * 128 : t % 2 * 128 + 128]

    pl.semaphore_wait(barrier, BAND - 1 + 6)

    def send1(t):
        return remote(bt.at[t], rs1.at[me], s1.at[t], r1.at[0], band=4 * t)

    for t in range(4):
        @pl.when(me != 4 * t)
        def _(t=t):
            send1(t).start()

        @pl.when(me == 4 * t)
        def _(t=t):
            rs1[me] = bt[t]

    loads[2].wait()
    pout[:, 0:GXY] = pot[0:16, :].astype(BF16)
    pex[...] = jnp.zeros(pex.shape, F32)
    for r in range(2):
        for c in range(6):
            pex[r * 6 + c : r * 6 + c + 1, :] = pot[16 + r : 17 + r, c * 384 : c * 384 + 384]
    pout[:, GXY : GXY + 384] = pex[...].astype(BF16)
    near = me // 6
    first = DEPTH * me - CZ * near

    def send_pot(half):
        return remote(
            pout, pin.at[half], sp.at[half], rp.at[half],
            slab=lax.rem(slab + SLAB - near - half, SLAB),
        )

    @pl.when(near != 0)
    def _():
        send_pot(0).start()

    @pl.when(near == 0)
    def _():
        pin[0] = pout[...]

    send_pot(1).start()

    tile = me // 4

    def send2(rel):
        return remote(tt.at[tile], tt.at[tile], s2.at[0], r2.at[tile], band=peer(rel))

    def start2(rel, carry):
        send2(rel).start()
        return carry

    @pl.when(lax.rem(me, 4) == 0)
    def _():
        take(r1.at[0], rs1.at[pl.ds(0, BAND - 1)])
        tt[tile] = jnp.sum(rs1[...], axis=0)
        lax.fori_loop(1, BAND, start2, 0)

    for d in range(DEPTH):
        part = tables.at[d, :, pl.ds(0, NPAIR)]
        pltpu.make_async_copy(part, part, tab_sem.at[d]).wait()
    for load in loads[3:]:
        load.wait()

    offset_row = root[...] - slab * CZ
    offset = column(offset_row)
    anchor = column(xy[...])
    species = column(kind[...])
    corner = anchor - GX * ((anchor.astype(F32) + 0.5) * (1.0 / GX)).astype(jnp.int32)
    lane = iota((DEPTH * ATOMS, GXY), 1)
    line = lane - GX * ((lane.astype(F32) + 0.5) * (1.0 / GX)).astype(jnp.int32)
    corner = jnp.broadcast_to(jnp.concatenate([corner] * DEPTH, axis=0), line.shape)
    anchor = jnp.concatenate([anchor] * DEPTH, axis=0)
    mine = jnp.broadcast_to(species, (ATOMS, ROWS)) == (iota((ATOMS, ROWS), 1) & 1)
    to_rows = jnp.where((iota((256, ROWS), 1) >> 1) == iota((256, ROWS), 0), 1.0, 0.0).astype(BF16)

    for t in range(4):
        @pl.when(me != 4 * t)
        def _(t=t):
            remote(tt.at[t], tt.at[t], s2.at[0], r2.at[t], band=4 * t).wait_recv()

    packed = jnp.concatenate(
        [
            jnp.concatenate([tt[0], tt[1]], axis=1),
            jnp.concatenate([tt[2], tt[3]], axis=1),
        ],
        axis=0,
    ).astype(BF16)
    left = jnp.where(mine, dot(packed, to_rows), 0.0).astype(BF16)
    terms = []
    for d in range(DEPTH):
        terms.append(
            jnp.concatenate([dot(left, rows_of(tables, d, c)) for c in range(TILES // 2)], axis=1)
        )
    placed = rotate(jnp.concatenate(terms, axis=0), anchor, False)
    placed = jnp.where(line >= corner, placed, pltpu.roll(placed, GXY - GX, 1))
    parts = split(placed, 2)
    window = jnp.zeros((WINDOW, GXY), F32)
    for d in range(DEPTH):
        onto = jnp.where(iota((WINDOW, ATOMS), 0) == offset_row + d, 1.0, 0.0).astype(BF16)
        for part in parts:
            window = window + dot(onto, part[d * ATOMS : (d + 1) * ATOMS])
    for j in range(OWNERS):
        ext[j, :, 0:WIDE] = window[0:16, j * WIDE : (j + 1) * WIDE].astype(BF16)
        ends = [window[16:24, j * WIDE + c * 128 : j * WIDE + c * 128 + 128] for c in range(3)]
        ends = jnp.concatenate([ends[0] + pltpu.roll(ends[1], 4, 0), ends[2]], axis=0)
        ext[j, :, WIDE : WIDE + 128] = ends.astype(BF16)

    def send3(j):
        return remote(ext.at[j], rs3.at[me], s3.at[j], r3.at[0], band=8 * j // 3)

    for j in range(OWNERS):
        @pl.when(me != 8 * j // 3)
        def _(j=j):
            send3(j).start()

        @pl.when(me == 8 * j // 3)
        def _(j=j):
            rs3[me] = ext[j]

    @pl.when(near != 0)
    def _():
        send_pot(0).wait_recv()

    send_pot(1).wait_recv()
    extra = []
    for half in range(2):
        packed_rows = pin[half, :, GXY : GXY + 384].astype(F32)
        for r in range(2):
            extra.append(
                jnp.concatenate([packed_rows[r * 6 + c : r * 6 + c + 1] for c in range(6)], axis=1)
            )
    extra = jnp.concatenate(extra + [jnp.zeros((12, GXY), F32)], axis=0).astype(BF16)
    planes = jnp.concatenate([pin[0, :, 0:GXY], pin[1, :, 0:GXY], extra], axis=0)
    picked = []
    for d in range(DEPTH):
        target = offset + (first + d)
        late = jnp.where(target >= CZ, 1, 0)
        row = target - CZ * late
        source = jnp.where(row < 16, 16 * late + row, 32 + 2 * late + row - 16)
        choose = jnp.where(
            iota((ATOMS, 48), 1) == jnp.broadcast_to(source, (ATOMS, 48)), 1.0, 0.0
        ).astype(BF16)
        picked.append(dot(choose, planes))
    turned = rotate(jnp.concatenate(picked, axis=0), anchor, True)
    turned = jnp.where(line < GX - corner, turned, pltpu.roll(turned, GX, 1))
    for d in range(DEPTH):
        boxes[d] = turned[d * ATOMS : (d + 1) * ATOMS].astype(BF16)

    mark = (3 * me + 7) // 8
    owner = jnp.logical_and(mark < OWNERS, 8 * mark // 3 == me)
    own = jnp.minimum(mark, OWNERS - 1)

    def send4(k):
        return remote(
            st.at[k], p4.at[k - 1], s4.at[k - 1], r4.at[k - 1], slab=lax.rem(slab + k, SLAB)
        )

    def send5(rel):
        return remote(ag.at[own], ag.at[own], s5.at[0], r5.at[own], band=peer(rel))

    def start5(rel, carry):
        send5(rel).start()
        return carry

    @pl.when(owner)
    def _():
        out_row = iota((4 * WINDOW, 256), 0)
        block = jnp.zeros(out_row.shape, jnp.int32)
        for k in (1, 2, 3):
            block = block + jnp.where(out_row >= k * WINDOW, 1, 0)
        out_row = out_row - WINDOW * block
        plane = jnp.where(out_row < CZ, out_row + CZ * block, -1)
        source = iota((4 * WINDOW, 256), 1)
        base = DEPTH * (source >> 4)
        source = source & 15
        gather = jnp.where(plane == base + source, 1.0, 0.0).astype(BF16)
        tails = [
            jnp.where(
                jnp.logical_and(source >> 2 == c, plane == base + 16 + (source & 3)), 1.0, 0.0
            ).astype(BF16)
            for c in range(3)
        ]
        take(r3.at[0], rs3.at[pl.ds(0, BAND - 1)])
        end = rs3[:, :, WIDE : WIDE + 128].reshape(256, 128)
        whole = dot(gather, rs3[:, :, 0:WIDE].reshape(256, WIDE))
        whole = whole + jnp.concatenate([dot(tails[c], end) for c in range(3)], axis=1)
        for k in range(4):
            st[k] = whole[k * WINDOW : (k + 1) * WINDOW]
        for k in (1, 2, 3):
            send4(k).start()

    sums = jnp.zeros((ATOMS, ROWS), F32)
    for d in range(DEPTH):
        for c in range(TILES // 2):
            sums = sums + dot_nt(boxes[d, :, 256 * c : 256 * c + 256], rows_of(tables, d, c))
    folded = jnp.zeros((ATOMS, 256), F32)
    for part in split(jnp.where(mine, sums, 0.0), 3):
        folded = folded + dot_nt(part, to_rows)
    for a in range(ATOMS):
        isnd[a] = folded[a : a + 1]

    def send6(rel):
        other = peer(rel)
        return remote(isnd.at[other], ircv.at[me], s6.at[0], r6.at[0], band=other)

    def start6(rel, carry):
        send6(rel).start()
        return carry

    lax.fori_loop(1, BAND, start6, 0)
    ircv[me] = isnd[me]

    @pl.when(owner)
    def _():
        for k in (1, 2, 3):
            send4(k).wait_recv()
        total = st[0] + p4[0] + p4[1] + p4[2]
        ends = [total[16:24, c * 128 : c * 128 + 128] for c in range(3)]
        ends = ends[0] + pltpu.roll(ends[1], 2, 0) + pltpu.roll(ends[2], 4, 0)
        ends = jnp.concatenate([ends, jnp.zeros_like(ends)], axis=0)
        ag[own, :, 0:WIDE] = total[0:16].astype(BF16)
        ag[own, :, WIDE : WIDE + 128] = ends.astype(BF16)
        lax.fori_loop(1, BAND, start5, 0)

    take(r6.at[0], ircv.at[pl.ds(0, BAND - 1)])
    ints[...] = jnp.sum(ircv[...], axis=0)

    for j in range(OWNERS):
        @pl.when(me != 8 * j // 3)
        def _(j=j):
            remote(ag.at[j], ag.at[j], s5.at[0], r5.at[j], band=8 * j // 3).wait_recv()

        dens[0:16, j * WIDE : (j + 1) * WIDE] = ag[j, :, 0:WIDE]
        ends = ag[j, :, WIDE : WIDE + 128].astype(F32)[0:8]
        for c in range(3):
            at = j * WIDE + c * 128
            tail = pltpu.roll(ends, 8 - 2 * c, 0) if c else ends
            tail = jnp.concatenate([tail, jnp.zeros_like(tail)], axis=0)
            dens[16:32, at : at + 128] = tail.astype(BF16)

    for t in range(4):
        @pl.when(me != 4 * t)
        def _(t=t):
            send1(t).wait_send()

    @pl.when(near != 0)
    def _():
        send_pot(0).wait_send()

    send_pot(1).wait_send()

    @pl.when(lax.rem(me, 4) == 0)
    def _():
        take(s2.at[0], rs1.at[pl.ds(0, BAND - 1)])

    for j in range(OWNERS):
        @pl.when(me != 8 * j // 3)
        def _(j=j):
            send3(j).wait_send()

    take(s6.at[0], ircv.at[pl.ds(0, BAND - 1)])

    @pl.when(owner)
    def _():
        for k in (1, 2, 3):
            send4(k).wait_send()
        take(s5.at[0], rs3.at[pl.ds(0, BAND - 1)])


def finish(rounded, sums, density, integrals):
    density[...] = rounded[...].astype(F32)[0:CZ]
    integrals[...] = sums[:, 0:NPAIR]


def shards(projections, occupation, augment_tables, box_root, box_xy, species, potential):
    pt = jnp.transpose(projections, (1, 2, 0)).reshape(NH * ATOMS, 256)
    tab = jnp.transpose(augment_tables.reshape(2, NPAIR, DEPTH, TILES, 128), (1, 2, 3, 0, 4))
    vmem = pl.BlockSpec(memory_space=pltpu.VMEM)
    dma = pltpu.SemaphoreType.DMA
    density, integrals = pl.pallas_call(
        kernel,
        out_shape=(
            jax.ShapeDtypeStruct((32, GXY), BF16),
            jax.ShapeDtypeStruct((1, 256), F32),
        ),
        in_specs=[pl.BlockSpec(memory_space=pltpu.HBM)] * 7,
        out_specs=(vmem, vmem),
        scratch_shapes=[
            pltpu.VMEM((NH * ATOMS, 256), BF16),
            pltpu.VMEM((1, 256), F32),
            pltpu.VMEM((1, ATOMS), jnp.int32),
            pltpu.VMEM((1, ATOMS), jnp.int32),
            pltpu.VMEM((1, ATOMS), jnp.int32),
            pltpu.VMEM((CZ, GXY), F32),
            pltpu.VMEM((DEPTH, TILES, PAD_P, 2, 128), BF16),
            pltpu.VMEM((4, 8, 128), F32),
            pltpu.VMEM((BAND, 8, 128), F32),
            pltpu.VMEM((4, 8, 128), F32),
            pltpu.VMEM((16, 384), F32),
            pltpu.VMEM((16, GXY + 384), BF16),
            pltpu.VMEM((2, 16, GXY + 384), BF16),
            pltpu.VMEM((DEPTH, ATOMS, GXY), BF16),
            pltpu.VMEM((OWNERS, 16, WIDE + 128), BF16),
            pltpu.VMEM((BAND, 16, WIDE + 128), BF16),
            pltpu.VMEM((4, WINDOW, WIDE), F32),
            pltpu.VMEM((3, WINDOW, WIDE), F32),
            pltpu.VMEM((OWNERS, 16, WIDE + 128), BF16),
            pltpu.VMEM((ATOMS, 1, 256), F32),
            pltpu.VMEM((BAND, 1, 256), F32),
            dma((6,)),
            dma((DEPTH,)),
            dma((4,)), dma((1,)),
            dma((1,)), dma((4,)),
            dma((2,)), dma((2,)),
            dma((OWNERS,)), dma((1,)),
            dma((3,)), dma((3,)),
            dma((1,)), dma((OWNERS,)),
            dma((1,)), dma((1,)),
        ],
        compiler_params=pltpu.CompilerParams(
            collective_id=0, has_side_effects=True, vmem_limit_bytes=56 << 20
        ),
    )(
        pt,
        occupation.reshape(1, 256),
        box_root.reshape(1, ATOMS),
        box_xy.reshape(1, ATOMS),
        species.reshape(1, ATOMS),
        potential,
        tab,
    )
    density, integrals = pl.pallas_call(
        finish,
        out_shape=(
            jax.ShapeDtypeStruct((CZ, GXY), F32),
            jax.ShapeDtypeStruct((1, NPAIR), F32),
        ),
        in_specs=[vmem] * 2,
        out_specs=(vmem, vmem),
        compiler_params=pltpu.CompilerParams(vmem_limit_bytes=56 << 20),
    )(density, integrals)
    return density, integrals.reshape(NPAIR, 1)


def solution(mesh):
    placed = (
        P("band", None, "slab"),
        P("band"),
        P(None, None, "band", None),
        P("slab"),
        P("slab"),
        P("slab"),
        P("slab", None),
    )
    return jax.shard_map(
        shards,
        mesh=mesh,
        in_specs=placed,
        out_specs=(P("slab", None), P(None, ("slab", "band"))),
        check_vma=False,
    )
```

```python
import jax
import jax.numpy as jnp
from jax import lax
from jax.experimental import pallas as pl
from jax.experimental.pallas import tpu as pltpu
from jax.sharding import PartitionSpec as P

GX = 48
GXY = 2304
NH = 18
NPAIR = 171
DEPTH = 3
CZ = 18
ATOMS = 16
BAND = 16
SLAB = 32
PAD_P = 176
ROWS = 2 * PAD_P
OWNERS = 6
WIDE = GXY // OWNERS
WINDOW = 24
TILES = 18
F32 = jnp.float32
BF16 = jnp.bfloat16
NT = (((1,), (1,)), ((), ()))


def iota(shape, axis):
    return lax.broadcasted_iota(jnp.int32, shape, axis)


def dot(a, b):
    return jnp.dot(a, b, preferred_element_type=F32)


def dot_nt(a, b):
    return lax.dot_general(a, b, NT, preferred_element_type=F32)


def split(x, terms):
    parts = []
    for _ in range(terms):
        part = x.astype(BF16)
        parts.append(part)
        x = x - part.astype(F32)
    return parts


def column(row):
    picked = jnp.where(iota((ATOMS, ATOMS), 0) == iota((ATOMS, ATOMS), 1), row.astype(F32), 0.0)
    return jnp.sum(picked, axis=1, keepdims=True).astype(jnp.int32)


def rows_of(tables, d, c):
    return jnp.concatenate(
        [tables[d, 2 * c].reshape(ROWS, 128), tables[d, 2 * c + 1].reshape(ROWS, 128)], axis=1
    )


def take(sem, landed):
    pltpu.make_async_copy(landed, landed, sem).wait()


def rotate(values, amount, left):
    amount = jnp.broadcast_to(amount, values.shape)
    for bit in range(12):
        step = 1 << bit
        turned = pltpu.roll(values, GXY - step if left else step, 1)
        values = jnp.where((amount & step) != 0, turned, values)
    return values


def remote(src, dst, send, recv, **where):
    return pltpu.make_async_remote_copy(
        src_ref=src,
        dst_ref=dst,
        send_sem=send,
        recv_sem=recv,
        device_id=where,
        device_id_type=pl.DeviceIdType.MESH,
    )


def kernel(
    pt_hbm, occ_hbm, root_hbm, xy_hbm, kind_hbm, pot_hbm, tab, ag, ints_hbm,
    pt, occ, root, xy, kind, pot, tables, bt, rs1, tt, pex, pout, pin, boxes, ext, rs3, st, p4, piece, ints, isnd, ircv,
    in_sem, out_sem, tab_sem, s1, r1, s2, r2, sp, rp, s3, r3, s4, r4, s5, r5, s6, r6,
):
    me = lax.axis_index("band")
    slab = lax.axis_index("slab")

    def peer(rel):
        return lax.rem(me + rel, BAND)

    loads = [
        pltpu.make_async_copy(src, dst, in_sem.at[n])
        for n, (src, dst) in enumerate(
            [(pt_hbm, pt), (occ_hbm, occ), (pot_hbm, pot), (root_hbm, root), (xy_hbm, xy), (kind_hbm, kind)]
        )
    ]
    loads[0].start()
    loads[1].start()
    barrier = pltpu.get_barrier_semaphore()

    def greet(rel, carry):
        pl.semaphore_signal(
            barrier, inc=1, device_id={"band": peer(rel)}, device_id_type=pl.DeviceIdType.MESH
        )
        return carry

    lax.fori_loop(1, BAND, greet, 0)
    for k in (1, 2, 3, SLAB - 3, SLAB - 2, SLAB - 1):
        pl.semaphore_signal(
            barrier, inc=1, device_id={"slab": lax.rem(slab + k, SLAB)},
            device_id_type=pl.DeviceIdType.MESH,
        )
    for load in loads[2:]:
        load.start()
    tables[:, :, NPAIR:PAD_P] = jnp.zeros((DEPTH, TILES, PAD_P - NPAIR, 2, 128), BF16)
    for d in range(DEPTH):
        for c in range(TILES):
            pltpu.make_async_copy(
                tab.at[:, d, c], tables.at[d, c, pl.ds(0, NPAIR)], tab_sem.at[d]
            ).start()

    size = NH * ATOMS
    same = (iota((size, size), 0) & 15) == (iota((size, size), 1) & 15)
    pair = iota((1, 256), 1)
    i_of = jnp.zeros((1, 256), jnp.int32)
    start = jnp.zeros((1, 256), jnp.int32)
    for i in range(1, NH):
        past = pair >= i * NH - i * (i - 1) // 2
        i_of = i_of + jnp.where(past, 1, 0)
        start = start + jnp.where(past, NH - i + 1, 0)
    j_of = pair - start + i_of
    pick_j = jnp.where((iota((size, 256), 0) >> 4) == j_of, 1.0, 0.0).astype(BF16)
    loads[0].wait()
    loads[1].wait()
    p = pt[...]
    weighted = split(p.astype(F32) * occ[...], 2)
    gram = dot_nt(weighted[0], p) + dot_nt(weighted[1], p)
    spread = jnp.zeros((size, 256), F32)
    for part in split(jnp.where(same, gram, 0.0), 2):
        spread = spread + dot(part, pick_j)
    partial = jnp.zeros((ATOMS, 256), F32)
    for i in range(NH):
        partial = partial + jnp.where(i_of == i, spread[i * ATOMS : (i + 1) * ATOMS], 0.0)
    partial = partial * jnp.where(i_of == j_of, 1.0, 2.0)
    for t in range(4):
        bt[t] = partial[t // 2 * 8 : t // 2 * 8 + 8, t % 2 * 128 : t % 2 * 128 + 128]

    pl.semaphore_wait(barrier, BAND - 1 + 6)

    def send1(t):
        return remote(bt.at[t], rs1.at[me], s1.at[t], r1.at[0], band=4 * t)

    for t in range(4):
        @pl.when(me != 4 * t)
        def _(t=t):
            send1(t).start()

        @pl.when(me == 4 * t)
        def _(t=t):
            rs1[me] = bt[t]

    loads[2].wait()
    pout[:, 0:GXY] = pot[0:16, :].astype(BF16)
    pex[...] = jnp.zeros(pex.shape, F32)
    for r in range(2):
        for c in range(6):
            pex[r * 6 + c : r * 6 + c + 1, :] = pot[16 + r : 17 + r, c * 384 : c * 384 + 384]
    pout[:, GXY : GXY + 384] = pex[...].astype(BF16)
    near = me // 6
    first = DEPTH * me - CZ * near

    def send_pot(half):
        return remote(
            pout, pin.at[half], sp.at[half], rp.at[half],
            slab=lax.rem(slab + SLAB - near - half, SLAB),
        )

    @pl.when(near != 0)
    def _():
        send_pot(0).start()

    @pl.when(near == 0)
    def _():
        pin[0] = pout[...]

    send_pot(1).start()

    tile = me // 4

    def send2(rel):
        return remote(tt.at[tile], tt.at[tile], s2.at[0], r2.at[tile], band=peer(rel))

    def start2(rel, carry):
        send2(rel).start()
        return carry

    @pl.when(lax.rem(me, 4) == 0)
    def _():
        take(r1.at[0], rs1.at[pl.ds(0, BAND - 1)])
        tt[tile] = jnp.sum(rs1[...], axis=0)
        lax.fori_loop(1, BAND, start2, 0)

    for d in range(DEPTH):
        part = tables.at[d, :, pl.ds(0, NPAIR)]
        pltpu.make_async_copy(part, part, tab_sem.at[d]).wait()
    for load in loads[3:]:
        load.wait()

    offset_row = root[...] - slab * CZ
    offset = column(offset_row)
    anchor = column(xy[...])
    species = column(kind[...])
    corner = anchor - GX * ((anchor.astype(F32) + 0.5) * (1.0 / GX)).astype(jnp.int32)
    lane = iota((DEPTH * ATOMS, GXY), 1)
    line = lane - GX * ((lane.astype(F32) + 0.5) * (1.0 / GX)).astype(jnp.int32)
    corner = jnp.broadcast_to(jnp.concatenate([corner] * DEPTH, axis=0), line.shape)
    anchor = jnp.concatenate([anchor] * DEPTH, axis=0)
    mine = jnp.broadcast_to(species, (ATOMS, ROWS)) == (iota((ATOMS, ROWS), 1) & 1)
    to_rows = jnp.where((iota((256, ROWS), 1) >> 1) == iota((256, ROWS), 0), 1.0, 0.0).astype(BF16)

    for t in range(4):
        @pl.when(me != 4 * t)
        def _(t=t):
            remote(tt.at[t], tt.at[t], s2.at[0], r2.at[t], band=4 * t).wait_recv()

    packed = jnp.concatenate(
        [
            jnp.concatenate([tt[0], tt[1]], axis=1),
            jnp.concatenate([tt[2], tt[3]], axis=1),
        ],
        axis=0,
    ).astype(BF16)
    left = jnp.where(mine, dot(packed, to_rows), 0.0).astype(BF16)
    terms = []
    for d in range(DEPTH):
        terms.append(
            jnp.concatenate([dot(left, rows_of(tables, d, c)) for c in range(TILES // 2)], axis=1)
        )
    placed = rotate(jnp.concatenate(terms, axis=0), anchor, False)
    placed = jnp.where(line >= corner, placed, pltpu.roll(placed, GXY - GX, 1))
    parts = split(placed, 2)
    window = jnp.zeros((WINDOW, GXY), F32)
    for d in range(DEPTH):
        onto = jnp.where(iota((WINDOW, ATOMS), 0) == offset_row + d, 1.0, 0.0).astype(BF16)
        for part in parts:
            window = window + dot(onto, part[d * ATOMS : (d + 1) * ATOMS])
    for j in range(OWNERS):
        ext[j, :, 0:WIDE] = window[0:16, j * WIDE : (j + 1) * WIDE].astype(BF16)
        ends = [window[16:24, j * WIDE + c * 128 : j * WIDE + c * 128 + 128] for c in range(3)]
        ends = jnp.concatenate([ends[0] + pltpu.roll(ends[1], 4, 0), ends[2]], axis=0)
        ext[j, :, WIDE : WIDE + 128] = ends.astype(BF16)

    def send3(j):
        return remote(ext.at[j], rs3.at[me], s3.at[j], r3.at[0], band=8 * j // 3)

    for j in range(OWNERS):
        @pl.when(me != 8 * j // 3)
        def _(j=j):
            send3(j).start()

        @pl.when(me == 8 * j // 3)
        def _(j=j):
            rs3[me] = ext[j]

    @pl.when(near != 0)
    def _():
        send_pot(0).wait_recv()

    send_pot(1).wait_recv()
    extra = []
    for half in range(2):
        packed_rows = pin[half, :, GXY : GXY + 384].astype(F32)
        for r in range(2):
            extra.append(
                jnp.concatenate([packed_rows[r * 6 + c : r * 6 + c + 1] for c in range(6)], axis=1)
            )
    extra = jnp.concatenate(extra + [jnp.zeros((12, GXY), F32)], axis=0).astype(BF16)
    planes = jnp.concatenate([pin[0, :, 0:GXY], pin[1, :, 0:GXY], extra], axis=0)
    picked = []
    for d in range(DEPTH):
        target = offset + (first + d)
        late = jnp.where(target >= CZ, 1, 0)
        row = target - CZ * late
        source = jnp.where(row < 16, 16 * late + row, 32 + 2 * late + row - 16)
        choose = jnp.where(
            iota((ATOMS, 48), 1) == jnp.broadcast_to(source, (ATOMS, 48)), 1.0, 0.0
        ).astype(BF16)
        picked.append(dot(choose, planes))
    turned = rotate(jnp.concatenate(picked, axis=0), anchor, True)
    turned = jnp.where(line < GX - corner, turned, pltpu.roll(turned, GX, 1))
    for d in range(DEPTH):
        boxes[d] = turned[d * ATOMS : (d + 1) * ATOMS].astype(BF16)

    mark = (3 * me + 7) // 8
    owner = jnp.logical_and(mark < OWNERS, 8 * mark // 3 == me)
    own = jnp.minimum(mark, OWNERS - 1)

    def send4(k):
        return remote(
            st.at[k], p4.at[k - 1], s4.at[k - 1], r4.at[k - 1], slab=lax.rem(slab + k, SLAB)
        )

    def send5(rel):
        return remote(piece, ag.at[own], s5.at[0], r5.at[own], band=peer(rel))

    def keep():
        return pltpu.make_async_copy(piece, ag.at[own], out_sem.at[0])

    def start5(rel, carry):
        send5(rel).start()
        return carry

    @pl.when(owner)
    def _():
        out_row = iota((4 * WINDOW, 256), 0)
        block = jnp.zeros(out_row.shape, jnp.int32)
        for k in (1, 2, 3):
            block = block + jnp.where(out_row >= k * WINDOW, 1, 0)
        out_row = out_row - WINDOW * block
        plane = jnp.where(out_row < CZ, out_row + CZ * block, -1)
        source = iota((4 * WINDOW, 256), 1)
        base = DEPTH * (source >> 4)
        source = source & 15
        gather = jnp.where(plane == base + source, 1.0, 0.0).astype(BF16)
        tails = [
            jnp.where(
                jnp.logical_and(source >> 2 == c, plane == base + 16 + (source & 3)), 1.0, 0.0
            ).astype(BF16)
            for c in range(3)
        ]
        take(r3.at[0], rs3.at[pl.ds(0, BAND - 1)])
        end = rs3[:, :, WIDE : WIDE + 128].reshape(256, 128)
        whole = dot(gather, rs3[:, :, 0:WIDE].reshape(256, WIDE))
        whole = whole + jnp.concatenate([dot(tails[c], end) for c in range(3)], axis=1)
        for k in range(4):
            st[k] = whole[k * WINDOW : (k + 1) * WINDOW]
        for k in (1, 2, 3):
            send4(k).start()

    sums = jnp.zeros((ATOMS, ROWS), F32)
    for d in range(DEPTH):
        for c in range(TILES // 2):
            sums = sums + dot_nt(boxes[d, :, 256 * c : 256 * c + 256], rows_of(tables, d, c))
    folded = jnp.zeros((ATOMS, 256), F32)
    for part in split(jnp.where(mine, sums, 0.0), 3):
        folded = folded + dot_nt(part, to_rows)
    for a in range(ATOMS):
        isnd[a] = folded[a : a + 1]

    def send6(rel):
        other = peer(rel)
        return remote(isnd.at[other], ircv.at[me], s6.at[0], r6.at[0], band=other)

    def start6(rel, carry):
        send6(rel).start()
        return carry

    lax.fori_loop(1, BAND, start6, 0)
    ircv[me] = isnd[me]

    @pl.when(owner)
    def _():
        for k in (1, 2, 3):
            send4(k).wait_recv()
        total = st[0] + p4[0] + p4[1] + p4[2]
        ends = [total[16:24, c * 128 : c * 128 + 128] for c in range(3)]
        ends = ends[0] + pltpu.roll(ends[1], 2, 0) + pltpu.roll(ends[2], 4, 0)
        ends = jnp.concatenate([ends, jnp.zeros_like(ends)], axis=0)
        piece[:, 0:WIDE] = total[0:16].astype(BF16)
        piece[:, WIDE : WIDE + 128] = ends.astype(BF16)
        lax.fori_loop(1, BAND, start5, 0)
        keep().start()

    take(r6.at[0], ircv.at[pl.ds(0, BAND - 1)])
    ints[...] = jnp.sum(ircv[...], axis=0)
    leave = pltpu.make_async_copy(ints, ints_hbm, out_sem.at[1])
    leave.start()

    for j in range(OWNERS):
        @pl.when(me != 8 * j // 3)
        def _(j=j):
            remote(piece, ag.at[j], s5.at[0], r5.at[j], band=8 * j // 3).wait_recv()

    for t in range(4):
        @pl.when(me != 4 * t)
        def _(t=t):
            send1(t).wait_send()

    @pl.when(near != 0)
    def _():
        send_pot(0).wait_send()

    send_pot(1).wait_send()

    @pl.when(lax.rem(me, 4) == 0)
    def _():
        take(s2.at[0], rs1.at[pl.ds(0, BAND - 1)])

    for j in range(OWNERS):
        @pl.when(me != 8 * j // 3)
        def _(j=j):
            send3(j).wait_send()

    take(s6.at[0], ircv.at[pl.ds(0, BAND - 1)])

    @pl.when(owner)
    def _():
        for k in (1, 2, 3):
            send4(k).wait_send()
        take(s5.at[0], rs3.at[pl.ds(0, BAND - 1)])
        keep().wait()

    leave.wait()


def finish(rounded, sums, density, integrals):
    for j in range(OWNERS):
        density[0:16, j * WIDE : (j + 1) * WIDE] = rounded[j, :, 0:WIDE].astype(F32)
        ends = rounded[j, :, WIDE : WIDE + 128].astype(F32)
        for c in range(3):
            at = j * WIDE + c * 128
            density[16:CZ, at : at + 128] = ends[2 * c : 2 * c + 2]
    integrals[...] = sums[:, 0:NPAIR]


def shards(projections, occupation, augment_tables, box_root, box_xy, species, potential):
    pt = jnp.transpose(projections, (1, 2, 0)).reshape(NH * ATOMS, 256)
    tab = jnp.transpose(augment_tables.reshape(2, NPAIR, DEPTH, TILES, 128), (1, 2, 3, 0, 4))
    vmem = pl.BlockSpec(memory_space=pltpu.VMEM)
    dma = pltpu.SemaphoreType.DMA
    density, integrals = pl.pallas_call(
        kernel,
        out_shape=(
            jax.ShapeDtypeStruct((OWNERS, 16, WIDE + 128), BF16),
            jax.ShapeDtypeStruct((1, 256), F32),
        ),
        in_specs=[pl.BlockSpec(memory_space=pltpu.HBM)] * 7,
        out_specs=(pl.BlockSpec(memory_space=pltpu.HBM),) * 2,
        scratch_shapes=[
            pltpu.VMEM((NH * ATOMS, 256), BF16),
            pltpu.VMEM((1, 256), F32),
            pltpu.VMEM((1, ATOMS), jnp.int32),
            pltpu.VMEM((1, ATOMS), jnp.int32),
            pltpu.VMEM((1, ATOMS), jnp.int32),
            pltpu.VMEM((CZ, GXY), F32),
            pltpu.VMEM((DEPTH, TILES, PAD_P, 2, 128), BF16),
            pltpu.VMEM((4, 8, 128), F32),
            pltpu.VMEM((BAND, 8, 128), F32),
            pltpu.VMEM((4, 8, 128), F32),
            pltpu.VMEM((16, 384), F32),
            pltpu.VMEM((16, GXY + 384), BF16),
            pltpu.VMEM((2, 16, GXY + 384), BF16),
            pltpu.VMEM((DEPTH, ATOMS, GXY), BF16),
            pltpu.VMEM((OWNERS, 16, WIDE + 128), BF16),
            pltpu.VMEM((BAND, 16, WIDE + 128), BF16),
            pltpu.VMEM((4, WINDOW, WIDE), F32),
            pltpu.VMEM((3, WINDOW, WIDE), F32),
            pltpu.VMEM((16, WIDE + 128), BF16),
            pltpu.VMEM((1, 256), F32),
            pltpu.VMEM((ATOMS, 1, 256), F32),
            pltpu.VMEM((BAND, 1, 256), F32),
            dma((6,)),
            dma((2,)),
            dma((DEPTH,)),
            dma((4,)), dma((1,)),
            dma((1,)), dma((4,)),
            dma((2,)), dma((2,)),
            dma((OWNERS,)), dma((1,)),
            dma((3,)), dma((3,)),
            dma((1,)), dma((OWNERS,)),
            dma((1,)), dma((1,)),
        ],
        compiler_params=pltpu.CompilerParams(
            collective_id=0, has_side_effects=True, vmem_limit_bytes=56 << 20
        ),
    )(
        pt,
        occupation.reshape(1, 256),
        box_root.reshape(1, ATOMS),
        box_xy.reshape(1, ATOMS),
        species.reshape(1, ATOMS),
        potential,
        tab,
    )
    density, integrals = pl.pallas_call(
        finish,
        out_shape=(
            jax.ShapeDtypeStruct((CZ, GXY), F32),
            jax.ShapeDtypeStruct((1, NPAIR), F32),
        ),
        in_specs=[vmem] * 2,
        out_specs=(vmem, vmem),
        compiler_params=pltpu.CompilerParams(vmem_limit_bytes=56 << 20),
    )(density, integrals)
    return density, integrals.reshape(NPAIR, 1)


def solution(mesh):
    placed = (
        P("band", None, "slab"),
        P("band"),
        P(None, None, "band", None),
        P("slab"),
        P("slab"),
        P("slab"),
        P("slab", None),
    )
    return jax.shard_map(
        shards,
        mesh=mesh,
        in_specs=placed,
        out_specs=(P("slab", None), P(None, ("slab", "band"))),
        check_vma=False,
    )
```
